512 devices in a mesh: shard: 128 (over z, y, core), rep: 4 (over x).
Axes of the slice: x: 4, y: 8, z: 8, core: 2. Of those that a mesh axis runs over, the one named last changes fastest.
Arguments:
- queries: bfloat16 [4, 128, 32, 128], P('rep', 'shard'), may hold values from -0.5 to 0.5
- candidates: int32 [4, 128, 64], P('rep', 'shard'), may hold values from 0 to 2047, all different within a row; in each aligned block of 128 rows (0 to 127, 128 to 255, ..., all dimensions but the last counted through in order) at most 8 rows name the same one
- codebook: bfloat16 [524288, 128], P(('shard', 'rep')), may hold values from -0.5 to 0.5
- bucket_weights: float32 [4], replicated, may hold values from -0.1 to 0.1
- centroid_ids: int32 [2048, 128], P('shard'), may hold values from 0 to 4095
- residual_codes: int32 [2048, 128, 128], P('shard'), may hold values from 0 to 3
- passage_lengths: int32 [2048], P('shard'), may hold values from 1 to 128, 196608 in all
Outputs:
- best_centroid: float32 [4, 128, 32], P('rep', 'shard')
- scores: float32 [4, 128, 64], P('rep', 'shard')
The draws below stay inside these ranges and needn't reach their ends.
Inputs may be any that keep to these rules, and one draw needn't show every extreme that they name: `candidates`: each query names 64 different passages. Within the 128 queries of one index of rep, no passage is named by more than 8 queries, a bound that some block reaches. `passage_lengths`: some passage has all 128 slots live.
All inputs are finite; a program needn't handle non-finite values. No bound on the sum of `passage_lengths` on one device may be relied on, other than what follows from the above.
Results may differ from the reference program's by a relative error of at most 0.00045.
Values may be sent and summed in bfloat16 or wider, within the bound.
A program may use at most 64 MiB of HBM per device.

```python
import math
import jax
import jax.numpy as jnp
import numpy as np
from jax import lax

DIM = 128
QT = 32
PT = 128
SHARD_CENT = 4096
NCENT = 524288
BUCKETS = 4
QG = 128
PDEV = 16
NPASS = 2048
NCAND = 64
MOST = 8
N_SHARD = 128
N_REP = 4


def place_ends(drawn, stream_key, smallest, largest):
    dims = drawn.shape
    spot = [jax.random.randint(jax.random.fold_in(stream_key, axis), (), 0, dims[axis]) for axis in range(len(dims))]
    drawn = drawn.at[tuple(spot)].set(smallest)
    longest = dims.index(max(dims))
    spot[longest] = (spot[longest] + 1) % dims[longest]
    return drawn.at[tuple(spot)].set(largest)


def level_of(stream_key, shape, shards, low, high):
    loudness = 1.0
    for dim, blocks in shards:
        draws = jax.random.uniform(jax.random.fold_in(jax.random.fold_in(stream_key, 6), dim), (blocks,), jnp.float32, low / len(shards), high / len(shards))
        loudness = loudness * jnp.repeat(jnp.exp(draws), shape[dim] // blocks).reshape((-1,) + (1,) * (len(shape) - 1 - dim))
    return loudness


def profile(number_of, total, most, slope):
    loads = [(1 << 20) // math.isqrt(grade ** slope) + 1 for grade in range(2, number_of + 1)]
    surplus, given = total - most - (number_of - 1), [1] * (number_of - 1)
    while surplus > 0:
        free = [i for i in range(number_of - 1) if given[i] < most]
        mass, budget = sum([loads[i] for i in free]), surplus
        for i in free:
            addition = min(most - given[i], max(1, budget * loads[i] // mass), surplus)
            given[i] = given[i] + addition
            surplus = surplus - addition
    return np.array([most] + given)


def uneven(rng, count, total, reach, slope):
    if count == 2:
        one = jax.random.randint(rng, (), max(1, total - reach), min(reach, total - 1) + 1)
        return jnp.stack([one, total - one])
    sizes = jnp.asarray(profile(count, total, reach, slope), jnp.int32)
    twos = (count - 1) // 2
    giver, receiver = sizes[1:1 + 2 * twos:2], sizes[2:2 + 2 * twos:2]
    margin = jnp.minimum(giver - 1, reach - receiver)
    moved = jax.random.randint(jax.random.fold_in(rng, 1), (twos,), 0, 1 << 20) % (margin + 1)
    sizes = sizes.at[1:1 + 2 * twos:2].set(giver - moved).at[2:2 + 2 * twos:2].set(receiver + moved)
    return sizes[jax.random.permutation(jax.random.fold_in(rng, 2), count)]


def assign_block(key, own, number, rows, amount, top, limit, lean):
    ranking = jax.random.permutation(key, amount)
    crowded, ordinary = load_shares(amount, rows * top, limit, lean, True), load_shares(amount, rows * top, limit, lean, False)
    places = jnp.arange(amount)

    def named(tallies, rotation):
        used = int((tallies > 0).sum())
        fixed = max(1, used // 4)
        passed = fixed + (places - fixed + rotation * (used - fixed)) % max(1, amount - fixed)
        return jnp.zeros((amount,), jnp.int32).at[ranking[jnp.where(places < fixed, places, passed)]].set(jnp.asarray(tallies, jnp.int32))

    tallies = jnp.where(number % 4 == 0, named(crowded, number // 4), named(ordinary, number - number // 4 - 1))
    mixed = jax.random.permutation(jax.random.fold_in(own, 3), amount)
    source_of, sink = mixed[0:amount // 2 * 2:2], mixed[1:amount // 2 * 2:2]
    room = jnp.minimum(tallies[source_of] - 1, limit - tallies[sink]) // 2
    room = jnp.where((source_of == ranking[0]) | (sink == ranking[0]) | (tallies[sink] == 0), 0, jnp.maximum(room, 0))
    passed = jax.random.randint(jax.random.fold_in(own, 4), (amount // 2,), 0, 1 << 20) % (room + 1)
    tallies = tallies.at[source_of].add(-passed).at[sink].add(passed)
    items = jnp.searchsorted(jnp.cumsum(tallies), jnp.arange(rows * top), side="right").astype(jnp.int32)
    table = items.reshape(top, rows).T
    table = table[jax.random.permutation(jax.random.fold_in(own, 1), rows)]
    rotation = jax.random.randint(jax.random.fold_in(own, 2), (rows, 1), 0, top)
    return jnp.take_along_axis(table, (jnp.arange(top)[None, :] + rotation) % top, axis=1)


def load_shares(amount, total, bound, lean, full):
    weights = [(1 << 20) // math.isqrt(standing ** lean) + 1 for standing in range(1, amount + 1)]
    largest = bound if full else min(bound, max(-(-total // amount), total * weights[0] // sum(weights)))
    least = 1 if total - largest >= amount - 1 else 0
    holding, rest = [largest] + [least] * (amount - 1), total - largest - least * (amount - 1)
    while rest > 0:
        movable = [i for i in range(1, amount) if holding[i] < largest] or [i for i in range(1, amount) if holding[i] < bound]
        whole, remaining = sum([weights[i] for i in movable]), rest
        for i in movable:
            extra = min(bound - holding[i], max(1, remaining * weights[i] // whole), rest)
            holding[i] = holding[i] + extra
            rest = rest - extra
    return np.array(holding)


def scatter_about(own_key, shape, spread, most, shards=(), kind=jnp.bfloat16):
    factor_of = level_of(own_key, shape, shards, -0.22, 0.18) if shards else 1.0
    result = jax.random.normal(own_key, shape, jnp.float32) * spread * factor_of
    return jnp.minimum(jnp.maximum(result, -most), most).astype(kind)


def setup_inputs(seed: int = 0) -> dict:
    streams_of = jax.random.split(jax.random.key(seed), 8)
    queries = scatter_about(streams_of[0], (N_REP, QG, QT, DIM), 0.088, 0.5, ((0, 4), (1, 128)))
    candidates_keys = jax.random.split(jax.random.fold_in(streams_of[1], 1), N_REP * QG // QG)
    candidates_turns = jax.random.permutation(jax.random.fold_in(streams_of[1], 3), N_REP * QG // QG)
    candidates = jax.vmap(lambda own, number: assign_block(jax.random.fold_in(streams_of[1], 2), own, number, QG, NPASS, NCAND, MOST, 2))(candidates_keys, candidates_turns).reshape((N_REP, QG, NCAND))
    codebook = scatter_about(streams_of[2], (NCENT, DIM), 0.088, 0.5, ((0, 512),))
    bucket_weights = jnp.clip(jax.random.uniform(streams_of[3], (BUCKETS,), jnp.float32, -0.1, 0.1), -0.1, 0.1)
    centroid_ids = place_ends(jax.random.randint(streams_of[4], (NPASS, PT), 0, SHARD_CENT), jax.random.fold_in(streams_of[4], 1), 0, SHARD_CENT - 1).astype(jnp.int32)
    residual_codes = place_ends(jax.random.randint(streams_of[5], (NPASS, PT, DIM), 0, BUCKETS), jax.random.fold_in(streams_of[5], 1), 0, BUCKETS - 1).astype(jnp.int32)
    passage_lengths = uneven(streams_of[6], NPASS, NPASS * PT * 3 // 4, PT, 1).astype(jnp.int32)
    return dict(queries=queries, candidates=candidates, codebook=codebook, bucket_weights=bucket_weights, centroid_ids=centroid_ids, residual_codes=residual_codes, passage_lengths=passage_lengths)


def reference(queries, candidates, codebook, bucket_weights, centroid_ids, residual_codes, passage_lengths):
    token_rows = queries.reshape(N_REP * QG * QT, DIM)
    books = codebook.reshape(N_SHARD, SHARD_CENT, DIM)

    def fold_step(running, shard_book):
        scored = jnp.dot(token_rows, shard_book.T, preferred_element_type=jnp.float32)
        return jnp.maximum(running, jnp.max(scored, axis=1)), None

    initial = jnp.full((N_REP * QG * QT,), -1e30, dtype=jnp.float32)
    best_flat, unused = lax.scan(fold_step, initial, books)
    best_centroid = best_flat.reshape(N_REP, QG, QT)

    owners = jnp.arange(NPASS, dtype=jnp.int32) // PDEV
    row_ids = (owners[:, None] * SHARD_CENT + centroid_ids).astype(jnp.int32)
    residual = jnp.take(bucket_weights, residual_codes)
    embedded = (jnp.take(codebook, row_ids, axis=0).astype(jnp.float32) + residual).astype(jnp.bfloat16)
    live_mask = jnp.arange(PT, dtype=jnp.int32)[None, :] < passage_lengths[:, None]

    def one_query(pair_args):
        query_tokens, cand_ids = pair_args
        picked = jnp.take(embedded, cand_ids, axis=0).astype(jnp.float32)
        picked_live = jnp.take(live_mask, cand_ids, axis=0)
        similar = jnp.einsum("td,cpd->ctp", query_tokens.astype(jnp.float32), picked)
        similar = jnp.where(picked_live[:, None, :], similar, -1e30)
        return jnp.sum(jnp.max(similar, axis=2), axis=1)

    scores = lax.map(one_query, (queries.reshape(N_REP * QG, QT, DIM), candidates.reshape(N_REP * QG, NCAND)))
    return best_centroid, scores.reshape(N_REP, QG, NCAND)
```

```python
import functools
import math

import jax
import jax.numpy as jnp
from jax import lax
from jax.experimental import pallas as pl
from jax.experimental.pallas import tpu as pltpu

FAR_BELOW = -1e30
MESH = pl.DeviceIdType.MESH
CORES = 2
SLOTS = 8
HALF = 16
DIMS = (((1,), (1,)), ((), ()))


def kernel(
    n, nx, query_ref, cand_ref, weight_ref, length_ref, id_ref, book_hbm, code_hbm,
    best_out, score_out,
    book, book32, toks, codes, extra32, fetched, emb, best_acc, pair_best,
    cand_row, cand_line, cand_all, hits, slot_vec, slot_smem, tiles, got1, line, got2,
    local_sem, s1, r1, s2, r2, s3, r3, sc1, rc1, sc2, rc2, sc3, rc3, sb, rb, sx, rx, sy, ry,
):
    quarter = book_hbm.shape[0]
    n_pass, pass_len = id_ref.shape
    n_cand = cand_ref.shape[1]
    side = CORES * n
    n_blocks = n * side
    n_query = CORES * n * n
    width = side * HALF
    lane_half = n * HALF

    shard = lax.axis_index("shard")
    rep = lax.axis_index("rep")
    c = lax.rem(shard, CORES)
    y = lax.rem(shard // CORES, n)
    z = shard // (CORES * n)

    def at(z_, y_, c_):
        return {"shard": (z_ * n + y_) * CORES + c_, "rep": rep}

    def near(me, k, count):
        step = (k + 1) // 2
        return lax.rem(jnp.where(lax.rem(k, 2) == 1, me + step, me + count - step), count)

    def rcopy(src, dst, send, recv, dev):
        return pltpu.make_async_remote_copy(
            src_ref=src, dst_ref=dst, send_sem=send, recv_sem=recv,
            device_id=dev, device_id_type=MESH,
        )

    sibling = at(z, y, 1 - c)

    def loop(low, high, body):
        def step(k, carry):
            body(k)
            return carry
        lax.fori_loop(low, high, step, 0)

    def blocks_a(z_, c_):
        return toks.at[pl.ds((z_ * CORES + c_) * n, n)]

    def blocks_b(y_, c_):
        return toks.at[pl.ds(n_blocks + (y_ * CORES + c_) * n, n)]

    own_rows = pl.ds(pl.multiple_of(rep * quarter, quarter), quarter)
    load_book = pltpu.make_async_copy(book_hbm, book.at[own_rows], local_sem.at[0])
    load_codes = pltpu.make_async_copy(code_hbm, codes, local_sem.at[1])
    load_book.start()
    load_codes.start()

    barrier = pltpu.get_barrier_semaphore()

    def greet(dev):
        pl.semaphore_signal(barrier, inc=1, device_id=dev, device_id_type=MESH)

    def greet_line(k):
        greet(at(z, near(y, k, n), c))
        greet(at(z, near(y, k, n), 1 - c))
        greet(at(near(z, k, n), y, c))

    loop(1, n, greet_line)
    loop(1, nx, lambda k: greet({"shard": shard, "rep": near(rep, k, nx)}))
    greet(sibling)

    toks[(z * CORES + c) * n + y] = query_ref[0:HALF]
    toks[n_blocks + (y * CORES + c) * n + z] = query_ref[HALF : 2 * HALF]
    cand_row[...] = jnp.full(cand_row.shape, -1, jnp.int32)
    cand_row[:, 0:n_cand] = cand_ref[...]
    cand_line[pl.ds(y, 1)] = cand_row[...].reshape(1, 1, 128)

    pl.semaphore_wait(barrier, 3 * (n - 1) + nx)

    def hop1_copies(k):
        ty, tz = near(y, k, n), near(z, k, n)
        block_a = toks.at[(z * CORES + c) * n + y]
        block_b = toks.at[n_blocks + (y * CORES + c) * n + z]
        return (
            rcopy(cand_line.at[y], cand_line.at[y], sc1.at[k], rc1.at[y], at(z, ty, c)),
            rcopy(block_a, block_a, s1.at[0, k], r1.at[0, y], at(z, ty, c)),
            rcopy(block_b, block_b, s1.at[1, k], r1.at[1, z], at(tz, y, c)),
        )

    def book_copy(k):
        return rcopy(
            book_hbm, book.at[own_rows], sb.at[k], rb.at[rep],
            {"shard": shard, "rep": near(rep, k, nx)},
        )

    def hop1_start(k):
        for copy in hop1_copies(k):
            copy.start()

    loop(1, n, hop1_start)
    loop(1, nx, lambda k: book_copy(k).start())

    load_codes.wait()

    def residual(p):
        part = codes[p]
        value = jnp.zeros(part.shape, jnp.float32)
        for level in range(weight_ref.shape[0]):
            value = jnp.where(part == level, weight_ref[level], value)
        extra32[p] = value

    loop(0, n_pass, residual)

    def hop1_wait(k):
        ty, tz = near(y, k, n), near(z, k, n)
        block_a = toks.at[(z * CORES + c) * n + ty]
        block_b = toks.at[n_blocks + (y * CORES + c) * n + tz]
        rcopy(cand_line.at[ty], cand_line.at[ty], sc1.at[k], rc1.at[ty], sibling).wait_recv()
        rcopy(block_a, block_a, s1.at[0, k], r1.at[0, ty], sibling).wait_recv()
        rcopy(block_b, block_b, s1.at[1, k], r1.at[1, tz], sibling).wait_recv()

    loop(1, n, hop1_wait)

    def cand_slab(z_, c_):
        return cand_all.at[pl.ds(c_ * n, n), pl.ds(z_, 1)]

    def hop2_copies(k):
        ty, tz = near(y, k, n), near(z, k, n)
        return (
            rcopy(blocks_a(z, c), blocks_a(z, c), s2.at[0, k], r2.at[0, z], at(tz, y, c)),
            rcopy(blocks_b(y, c), blocks_b(y, c), s2.at[1, k], r2.at[1, y], at(z, ty, c)),
            rcopy(cand_line, cand_slab(z, c), sc2.at[k], rc2.at[z], at(tz, y, c)),
        )

    def hop2_start(k):
        for copy in hop2_copies(k):
            copy.start()

    loop(1, n, hop2_start)
    own_cands = pltpu.make_async_copy(cand_line, cand_slab(z, c), local_sem.at[2])
    own_cands.start()

    def pass_on(k, half):
        if half == 0:
            zk = near(z, k, n)
            return rcopy(blocks_a(zk, c), blocks_a(zk, c), s3.at[0, k], r3.at[0, zk], sibling)
        yk = near(y, k, n)
        return rcopy(blocks_b(yk, c), blocks_b(yk, c), s3.at[1, k], r3.at[1, yk], sibling)

    pass_on(0, 0).start()
    pass_on(0, 1).start()
    own_cands.wait()

    def tile_best(tile, first_row, fresh):
        token = toks[pl.ds(tile * side, side)].reshape(width, toks.shape[2])
        part = book[pl.ds(pl.multiple_of(first_row, quarter), quarter)]
        scored = lax.dot_general(part, token, DIMS, preferred_element_type=jnp.float32)
        top = jnp.max(scored.reshape(quarter // 8, 8, width), axis=0)
        best_acc[tile] = top if fresh else jnp.maximum(best_acc[tile], top)

    def widen(r):
        span = pl.ds(pl.multiple_of(r * quarter, quarter), quarter)
        book32[span] = book[span].astype(jnp.float32)

    load_book.wait()
    widen(rep)

    def own_pair(k):
        zk, yk = near(z, k, n), near(y, k, n)
        other_a, other_b = blocks_a(zk, 1 - c), blocks_b(yk, 1 - c)
        rcopy(other_a, other_a, s3.at[0, k], r3.at[0, zk], sibling).wait_recv()
        rcopy(other_b, other_b, s3.at[1, k], r3.at[1, yk], sibling).wait_recv()
        tile_best(zk, rep * quarter, True)
        tile_best(n + yk, rep * quarter, True)

    def arrive(k):
        zk, yk = near(z, k, n), near(y, k, n)
        rcopy(blocks_a(zk, c), blocks_a(zk, c), s2.at[0, k], r2.at[0, zk], sibling).wait_recv()
        pass_on(k, 0).start()
        rcopy(blocks_b(yk, c), blocks_b(yk, c), s2.at[1, k], r2.at[1, yk], sibling).wait_recv()
        pass_on(k, 1).start()
        own_pair(k - 1)

    loop(1, n, arrive)

    def cands_wait(k):
        zk = near(z, k, n)
        rcopy(cand_line, cand_slab(zk, c), sc2.at[k], rc2.at[zk], sibling).wait_recv()

    loop(1, n, cands_wait)

    def cand_core(c_):
        return cand_all.at[pl.ds(c_ * n, n)]

    hand_cands = rcopy(cand_core(c), cand_core(c), sc3.at[0], rc3.at[0], sibling)
    hand_cands.start()
    own_pair(n - 1)

    rcopy(cand_core(1 - c), cand_core(1 - c), sc3.at[0], rc3.at[0], sibling).wait_recv()
    cand_t = jnp.transpose(cand_all[...].reshape(n_query, 128))[0:n_cand]
    first_pass = shard * n_pass
    for p in range(n_pass):
        hits[p : p + 1, :] = jnp.max(
            jnp.where(cand_t == first_pass + p, 1.0, 0.0), axis=0, keepdims=True
        )
    hit = hits[...]
    before = (
        lax.broadcasted_iota(jnp.int32, (n_query, n_query), 0)
        < lax.broadcasted_iota(jnp.int32, (n_query, n_query), 1)
    ).astype(jnp.bfloat16)
    rank = jnp.dot(hit.astype(jnp.bfloat16), before, preferred_element_type=jnp.float32)
    rank = jnp.where(hit > 0.5, rank, -1.0)
    bits = n.bit_length() - 1
    q_index = lax.broadcasted_iota(jnp.int32, (n_pass, n_query), 1)
    q_z = q_index & (n - 1)
    q_y = (q_index >> bits) & (n - 1)
    q_c = q_index >> (2 * bits)
    at_a = ((q_z * CORES + q_c) * n + q_y).astype(jnp.float32)
    at_b = ((q_y * CORES + q_c) * n + q_z + n_blocks).astype(jnp.float32)
    lane = lax.broadcasted_iota(jnp.int32, (n_pass, 128), 1)
    slots = jnp.zeros((n_pass, 128), jnp.float32)
    for k in range(SLOTS):
        mine = rank == float(k)
        slots = jnp.where(
            lane == k, jnp.sum(jnp.where(mine, at_a, 0.0), axis=1, keepdims=True), slots
        )
        slots = jnp.where(
            lane == SLOTS + k, jnp.sum(jnp.where(mine, at_b, 0.0), axis=1, keepdims=True), slots
        )
    slot_vec[...] = slots.astype(jnp.int32)
    to_smem = pltpu.make_async_copy(slot_vec, slot_smem, local_sem.at[3])
    to_smem.start()

    def other_quarter(k):
        r = near(rep, k, nx)
        span = pl.ds(pl.multiple_of(r * quarter, quarter), quarter)
        rcopy(book_hbm, book.at[span], sb.at[k], rb.at[r], sibling).wait_recv()
        widen(r)

        def half(h):
            for t in range(n):
                tile_best(h * n + t, r * quarter, False)

        loop(0, 2, half)

    loop(1, nx, other_quarter)
    to_smem.wait()

    group = 32

    def fetch(i):
        p = i // (pass_len // group)
        s0 = lax.rem(i, pass_len // group) * group
        for u in range(group):
            row = id_ref[p, s0 + u]
            fetched[pl.ds(i * group + u, 1)] = book32[pl.ds(row, 1)]

    loop(0, n_pass * pass_len // group, fetch)

    def decode(p):
        span = pl.ds(pl.multiple_of(p * pass_len, pass_len), pass_len)
        emb[span] = (fetched[span] + extra32[p]).astype(jnp.bfloat16)

    loop(0, n_pass, decode)

    slot_iota = lax.broadcasted_iota(jnp.int32, (pass_len, SLOTS * 2 * HALF), 0)

    def score(i):
        for u in range(4):
            p = i * 4 + u
            parts = []
            for k in range(SLOTS):
                parts.append(toks[jnp.clip(slot_smem[p, k], 0, n_blocks - 1)])
                parts.append(
                    toks[jnp.clip(slot_smem[p, SLOTS + k], n_blocks, 2 * n_blocks - 1)]
                )
            picked = jnp.concatenate(parts, axis=0)
            span = pl.ds(pl.multiple_of(p * pass_len, pass_len), pass_len)
            similar = lax.dot_general(
                emb[span], picked, DIMS, preferred_element_type=jnp.float32
            )
            similar = jnp.where(slot_iota < length_ref[p], similar, FAR_BELOW)
            pair_best[pl.ds(p, 1)] = jnp.max(similar, axis=0, keepdims=True)

    loop(0, n_pass // 4, score)

    tok_of = lax.broadcasted_iota(jnp.int32, (SLOTS * 2 * HALF, 128), 0) >> 5
    col_of = lax.broadcasted_iota(jnp.int32, (SLOTS * 2 * HALF, 128), 1)
    ones = (tok_of == col_of).astype(jnp.float32)
    slot_score = jnp.dot(
        pair_best[...], ones, preferred_element_type=jnp.float32,
        precision=lax.Precision.HIGHEST,
    )
    table = jnp.zeros((n_pass, n_query), jnp.float32)
    for k in range(SLOTS):
        table = jnp.where(rank == float(k), slot_score[:, k : k + 1], table)
    chosen = jnp.full((n_cand, n_query), FAR_BELOW, jnp.float32)
    for p in range(n_pass):
        chosen = jnp.where(cand_t == first_pass + p, table[p : p + 1, :], chosen)
    chosen = jnp.transpose(
        jnp.concatenate([chosen, jnp.full((128 - n_cand, n_query), FAR_BELOW, jnp.float32)], axis=0)
    )

    best = jnp.max(best_acc[...], axis=1)
    row_of = lax.broadcasted_iota(jnp.int32, (n, 128), 0)
    lane_of = lax.broadcasted_iota(jnp.int32, (n, 128), 1)
    in_a = (lane_of >= n_cand) & (lane_of < n_cand + HALF)
    in_b = (lane_of >= n_cand + HALF) & (lane_of < n_cand + 2 * HALF)

    def fit(part):
        if lane_half == 128:
            return part
        return jnp.concatenate([part, jnp.full((n, 128 - lane_half), FAR_BELOW, jnp.float32)], axis=1)

    for c_ in range(CORES):
        cols = slice(c_ * lane_half, (c_ + 1) * lane_half)
        best_a = fit(best[0:n, cols])
        best_b = fit(best[n : 2 * n, cols])
        for y_ in range(n):
            shift = (n_cand - y_ * HALF) % 128
            part_a = pltpu.roll(best_a, shift, 1) if shift else best_a
            part_b = jnp.where(
                (lane_of >> 4) == row_of, jnp.broadcast_to(best_b[y_ : y_ + 1], (n, 128)), FAR_BELOW
            )
            for step in (64, 32, 16):
                part_b = jnp.maximum(part_b, pltpu.roll(part_b, step, 1))
            t = c_ * n + y_
            tile = chosen[t * n : (t + 1) * n]
            tiles[t] = jnp.where(in_a, part_a, jnp.where(in_b, part_b, tile))

    me = c * n + y

    def merge1_copy(k, c_):
        ty = near(y, k, n)
        return rcopy(
            tiles.at[c_ * n + ty], got1.at[me], sx.at[c_ * n + ty], rx.at[me], at(z, ty, c_)
        )

    def merge1_start(k):
        merge1_copy(k, c).start()
        merge1_copy(k, 1 - c).start()

    loop(1, n, merge1_start)
    merge1_copy(0, 1 - c).start()

    def from1(k, c_):
        t = c_ * n + near(y, k, n)
        rcopy(tiles.at[t], got1.at[t], sx.at[t], rx.at[t], sibling).wait_recv()
        return got1[t]

    merged = lax.fori_loop(
        1, n,
        lambda k, acc: jnp.maximum(acc, jnp.maximum(from1(k, c), from1(k, 1 - c))),
        tiles[me],
    )
    merged = jnp.maximum(merged, from1(0, 1 - c))
    line[...] = merged

    def merge2_copy(k):
        tz = near(z, k, n)
        return rcopy(line.at[pl.ds(tz, 1)], got2.at[pl.ds(z, 1)], sy.at[k], ry.at[z], at(tz, y, c))

    loop(1, n, lambda k: merge2_copy(k).start())

    def from2(k, acc):
        tz = near(z, k, n)
        row = got2.at[pl.ds(tz, 1)]
        rcopy(row, row, sy.at[k], ry.at[tz], sibling).wait_recv()
        return jnp.maximum(acc, got2[pl.ds(tz, 1)])

    final = lax.fori_loop(1, n, from2, line[pl.ds(z, 1)])
    score_out[...] = final[:, 0:n_cand]
    best_out[...] = pltpu.roll(final, 128 - n_cand, 1)[:, 0 : 2 * HALF]

    def sent(k):
        for copy in hop1_copies(k) + hop2_copies(k):
            copy.wait_send()
        pass_on(k, 0).wait_send()
        pass_on(k, 1).wait_send()
        merge1_copy(k, c).wait_send()
        merge1_copy(k, 1 - c).wait_send()
        merge2_copy(k).wait_send()

    loop(1, n, sent)
    loop(1, nx, lambda k: book_copy(k).wait_send())
    pass_on(0, 0).wait_send()
    pass_on(0, 1).wait_send()
    hand_cands.wait_send()
    merge1_copy(0, 1 - c).wait_send()


def on_device(
    queries, candidates, codebook, bucket_weights, centroid_ids, residual_codes, passage_lengths, sizes
):
    n, nx = sizes
    query_len, width = queries.shape[2:]
    n_cand = candidates.shape[2]
    quarter = codebook.shape[0]
    n_pass, pass_len = centroid_ids.shape
    n_query = CORES * n * n
    tile_width = CORES * n * HALF
    vmem = pl.BlockSpec(memory_space=pltpu.VMEM)
    smem = pl.BlockSpec(memory_space=pltpu.SMEM)
    hbm = pl.BlockSpec(memory_space=pl.ANY)
    dma = pltpu.SemaphoreType.DMA
    f32, bf16, i32 = jnp.float32, jnp.bfloat16, jnp.int32
    best, scores = pl.pallas_call(
        functools.partial(kernel, n, nx),
        out_shape=(
            jax.ShapeDtypeStruct((1, query_len), f32),
            jax.ShapeDtypeStruct((1, n_cand), f32),
        ),
        in_specs=[vmem, vmem, smem, smem, smem, hbm, hbm],
        out_specs=(vmem, vmem),
        scratch_shapes=[
            pltpu.VMEM((nx * quarter, width), bf16),
            pltpu.VMEM((nx * quarter, width), f32),
            pltpu.VMEM((2 * n_query, HALF, width), bf16),
            pltpu.VMEM(residual_codes.shape, i32),
            pltpu.VMEM(residual_codes.shape, f32),
            pltpu.VMEM((n_pass * pass_len, width), f32),
            pltpu.VMEM((n_pass * pass_len, width), bf16),
            pltpu.VMEM((2 * n, 8, tile_width), f32),
            pltpu.VMEM((n_pass, SLOTS * 2 * HALF), f32),
            pltpu.VMEM((1, 128), i32),
            pltpu.VMEM((n, 1, 128), i32),
            pltpu.VMEM((CORES * n, n, 128), i32),
            pltpu.VMEM((n_pass, n_query), f32),
            pltpu.VMEM((n_pass, 128), i32),
            pltpu.SMEM((n_pass, 128), i32),
            pltpu.VMEM((CORES * n, n, 128), f32),
            pltpu.VMEM((CORES * n, n, 128), f32),
            pltpu.VMEM((n, 128), f32),
            pltpu.VMEM((n, 128), f32),
            dma((4,)),
            dma((2, n)), dma((2, n)),
            dma((2, n)), dma((2, n)),
            dma((2, n)), dma((2, n)),
            dma((n,)), dma((n,)),
            dma((n,)), dma((n,)),
            dma((1,)), dma((1,)),
            dma((nx,)), dma((nx,)),
            dma((CORES * n,)), dma((CORES * n,)),
            dma((n,)), dma((n,)),
        ],
        compiler_params=pltpu.CompilerParams(
            collective_id=0, has_side_effects=True, vmem_limit_bytes=40 << 20
        ),
        cost_estimate=pl.CostEstimate(flops=4 << 30, bytes_accessed=2 << 20, transcendentals=0),
        name="late_interaction",
    )(
        queries.reshape(query_len, width), candidates.reshape(1, n_cand), bucket_weights,
        passage_lengths, centroid_ids, codebook, residual_codes,
    )
    return best.reshape(1, 1, query_len), scores.reshape(1, 1, n_cand)


def solution(mesh):
    from jax.sharding import PartitionSpec as P

    nx = mesh.shape["rep"]
    n = math.isqrt(mesh.shape["shard"] // CORES)
    in_specs = (
        P("rep", "shard", None, None),
        P("rep", "shard", None),
        P(("shard", "rep"), None),
        P(),
        P("shard", None),
        P("shard", None, None),
        P("shard"),
    )
    out_specs = (P("rep", "shard", None), P("rep", "shard", None))
    return jax.shard_map(
        functools.partial(on_device, sizes=(n, nx)),
        mesh=mesh, in_specs=in_specs, out_specs=out_specs, check_vma=False,
    )
```

```python
import functools
import math

import jax
import jax.numpy as jnp
from jax import lax
from jax.experimental import pallas as pl
from jax.experimental.pallas import tpu as pltpu

FAR_BELOW = -1e30
MESH = pl.DeviceIdType.MESH
CORES = 2
SLOTS = 8
HALF = 16
DIMS = (((1,), (1,)), ((), ()))


def kernel(
    n, nx, query_hbm, cand_hbm, weight_hbm, length_hbm, id_hbm, book_hbm, code_hbm,
    best_out, score_out,
    query_ref, cand_ref, weight_ref, length_ref, id_ref,
    book, book32, toks, codes, extra32, fetched, emb, best_acc, pair_best,
    cand_row, cand_line, cand_all, hits, slot_vec, slot_smem, tiles, got1, line, got2,
    local_sem, s1, r1, s2, r2, s3, r3, sc1, rc1, sc2, rc2, sc3, rc3, sb, rb, sx, rx, sy, ry,
):
    quarter = book_hbm.shape[0]
    n_pass, pass_len = id_ref.shape
    n_cand = cand_ref.shape[1]
    side = CORES * n
    n_blocks = n * side
    n_query = CORES * n * n
    width = side * HALF
    lane_half = n * HALF

    shard = lax.axis_index("shard")
    rep = lax.axis_index("rep")
    c = lax.rem(shard, CORES)
    y = lax.rem(shard // CORES, n)
    z = shard // (CORES * n)

    def at(z_, y_, c_):
        return {"shard": (z_ * n + y_) * CORES + c_, "rep": rep}

    def near(me, k, count):
        step = (k + 1) // 2
        return lax.rem(jnp.where(lax.rem(k, 2) == 1, me + step, me + count - step), count)

    def rcopy(src, dst, send, recv, dev):
        return pltpu.make_async_remote_copy(
            src_ref=src, dst_ref=dst, send_sem=send, recv_sem=recv,
            device_id=dev, device_id_type=MESH,
        )

    sibling = at(z, y, 1 - c)

    def loop(low, high, body):
        def step(k, carry):
            body(k)
            return carry
        lax.fori_loop(low, high, step, 0)

    def blocks_a(z_, c_):
        return toks.at[pl.ds((z_ * CORES + c_) * n, n)]

    def blocks_b(y_, c_):
        return toks.at[pl.ds(n_blocks + (y_ * CORES + c_) * n, n)]

    own_rows = pl.ds(pl.multiple_of(rep * quarter, quarter), quarter)
    load_book = pltpu.make_async_copy(book_hbm, book.at[own_rows], local_sem.at[0])
    load_codes = pltpu.make_async_copy(code_hbm, codes, local_sem.at[1])
    small = [
        pltpu.make_async_copy(source, target, local_sem.at[4 + i])
        for i, (source, target) in enumerate((
            (query_hbm, query_ref), (cand_hbm, cand_ref), (weight_hbm, weight_ref),
            (length_hbm, length_ref), (id_hbm, id_ref),
        ))
    ]
    for copy in small:
        copy.start()
    load_book.start()
    load_codes.start()

    barrier = pltpu.get_barrier_semaphore()

    def greet(dev):
        pl.semaphore_signal(barrier, inc=1, device_id=dev, device_id_type=MESH)

    def greet_line(k):
        greet(at(z, near(y, k, n), c))
        greet(at(z, near(y, k, n), 1 - c))
        greet(at(near(z, k, n), y, c))

    loop(1, n, greet_line)
    loop(1, nx, lambda k: greet({"shard": shard, "rep": near(rep, k, nx)}))
    greet(sibling)

    for copy in small:
        copy.wait()
    toks[(z * CORES + c) * n + y] = query_ref[0:HALF]
    toks[n_blocks + (y * CORES + c) * n + z] = query_ref[HALF : 2 * HALF]
    cand_row[...] = jnp.full(cand_row.shape, -1, jnp.int32)
    cand_row[:, 0:n_cand] = cand_ref[...]
    cand_line[pl.ds(y, 1)] = cand_row[...].reshape(1, 1, 128)

    pl.semaphore_wait(barrier, 3 * (n - 1) + nx)

    def hop1_copies(k):
        ty, tz = near(y, k, n), near(z, k, n)
        block_a = toks.at[(z * CORES + c) * n + y]
        block_b = toks.at[n_blocks + (y * CORES + c) * n + z]
        return (
            rcopy(cand_line.at[y], cand_line.at[y], sc1.at[k], rc1.at[y], at(z, ty, c)),
            rcopy(block_a, block_a, s1.at[0, k], r1.at[0, y], at(z, ty, c)),
            rcopy(block_b, block_b, s1.at[1, k], r1.at[1, z], at(tz, y, c)),
        )

    def book_copy(k):
        return rcopy(
            book_hbm, book.at[own_rows], sb.at[k], rb.at[rep],
            {"shard": shard, "rep": near(rep, k, nx)},
        )

    def hop1_start(k):
        for copy in hop1_copies(k):
            copy.start()

    loop(1, n, hop1_start)
    loop(1, nx, lambda k: book_copy(k).start())

    load_codes.wait()

    def residual(p):
        part = codes[p]
        value = jnp.zeros(part.shape, jnp.float32)
        for level in range(weight_ref.shape[0]):
            value = jnp.where(part == level, weight_ref[level], value)
        extra32[p] = value

    loop(0, n_pass, residual)

    def hop1_wait(k):
        ty, tz = near(y, k, n), near(z, k, n)
        block_a = toks.at[(z * CORES + c) * n + ty]
        block_b = toks.at[n_blocks + (y * CORES + c) * n + tz]
        rcopy(cand_line.at[ty], cand_line.at[ty], sc1.at[k], rc1.at[ty], sibling).wait_recv()
        rcopy(block_a, block_a, s1.at[0, k], r1.at[0, ty], sibling).wait_recv()
        rcopy(block_b, block_b, s1.at[1, k], r1.at[1, tz], sibling).wait_recv()

    loop(1, n, hop1_wait)

    def cand_slab(z_, c_):
        return cand_all.at[pl.ds(c_ * n, n), pl.ds(z_, 1)]

    def hop2_copies(k):
        ty, tz = near(y, k, n), near(z, k, n)
        return (
            rcopy(blocks_a(z, c), blocks_a(z, c), s2.at[0, k], r2.at[0, z], at(tz, y, c)),
            rcopy(blocks_b(y, c), blocks_b(y, c), s2.at[1, k], r2.at[1, y], at(z, ty, c)),
            rcopy(cand_line, cand_slab(z, c), sc2.at[k], rc2.at[z], at(tz, y, c)),
        )

    def hop2_start(k):
        for copy in hop2_copies(k):
            copy.start()

    loop(1, n, hop2_start)
    own_cands = pltpu.make_async_copy(cand_line, cand_slab(z, c), local_sem.at[2])
    own_cands.start()

    def pass_on(k, half):
        if half == 0:
            zk = near(z, k, n)
            return rcopy(blocks_a(zk, c), blocks_a(zk, c), s3.at[0, k], r3.at[0, zk], sibling)
        yk = near(y, k, n)
        return rcopy(blocks_b(yk, c), blocks_b(yk, c), s3.at[1, k], r3.at[1, yk], sibling)

    pass_on(0, 0).start()
    pass_on(0, 1).start()
    own_cands.wait()

    def span_of(r):
        return pl.ds(pl.multiple_of(r * quarter, quarter), quarter)

    def best_of(tile, r):
        token = toks[pl.ds(tile * side, side)].reshape(width, toks.shape[2])
        scored = lax.dot_general(book[span_of(r)], token, DIMS, preferred_element_type=jnp.float32)
        return jnp.max(scored.reshape(quarter // 8, 8, width), axis=0)

    def widen(r):
        book32[span_of(r)] = book[span_of(r)].astype(jnp.float32)

    def take_quarter(k):
        r = near(rep, k, nx)
        span = book.at[span_of(r)]
        rcopy(book_hbm, span, sb.at[k], rb.at[r], sibling).wait_recv()
        widen(r)

    def pair(k):
        zk, yk = near(z, k, n), near(y, k, n)
        other_a, other_b = blocks_a(zk, 1 - c), blocks_b(yk, 1 - c)
        rcopy(other_a, other_a, s3.at[0, k], r3.at[0, zk], sibling).wait_recv()
        rcopy(other_b, other_b, s3.at[1, k], r3.at[1, yk], sibling).wait_recv()
        for tile in (zk, n + yk):
            top = best_of(tile, rep)
            for j in range(1, nx - 1):
                top = jnp.maximum(top, best_of(tile, near(rep, j, nx)))
            best_acc[tile] = top

    def forward(k):
        zk, yk = near(z, k, n), near(y, k, n)
        rcopy(blocks_a(zk, c), blocks_a(zk, c), s2.at[0, k], r2.at[0, zk], sibling).wait_recv()
        pass_on(k, 0).start()
        rcopy(blocks_b(yk, c), blocks_b(yk, c), s2.at[1, k], r2.at[1, yk], sibling).wait_recv()
        pass_on(k, 1).start()

    load_book.wait()
    widen(rep)
    forward(1)
    loop(1, nx - 1, take_quarter)

    def arrive(k):
        forward(k)
        pair(k - 2)

    loop(2, n, arrive)

    def cands_wait(k):
        zk = near(z, k, n)
        rcopy(cand_line, cand_slab(zk, c), sc2.at[k], rc2.at[zk], sibling).wait_recv()

    loop(1, n, cands_wait)

    def cand_core(c_):
        return cand_all.at[pl.ds(c_ * n, n)]

    hand_cands = rcopy(cand_core(c), cand_core(c), sc3.at[0], rc3.at[0], sibling)
    hand_cands.start()
    loop(n - 2, n, pair)

    rcopy(cand_core(1 - c), cand_core(1 - c), sc3.at[0], rc3.at[0], sibling).wait_recv()
    cand_t = jnp.transpose(cand_all[...].reshape(n_query, 128))[0:n_cand]
    first_pass = shard * n_pass
    for p in range(n_pass):
        hits[p : p + 1, :] = jnp.max(
            jnp.where(cand_t == first_pass + p, 1.0, 0.0), axis=0, keepdims=True
        )
    hit = hits[...]
    before = (
        lax.broadcasted_iota(jnp.int32, (n_query, n_query), 0)
        < lax.broadcasted_iota(jnp.int32, (n_query, n_query), 1)
    ).astype(jnp.bfloat16)
    rank = jnp.dot(hit.astype(jnp.bfloat16), before, preferred_element_type=jnp.float32)
    rank = jnp.where(hit > 0.5, rank, -1.0)
    bits = n.bit_length() - 1
    q_index = lax.broadcasted_iota(jnp.int32, (n_pass, n_query), 1)
    q_z = q_index & (n - 1)
    q_y = (q_index >> bits) & (n - 1)
    q_c = q_index >> (2 * bits)
    at_a = ((q_z * CORES + q_c) * n + q_y).astype(jnp.float32)
    at_b = ((q_y * CORES + q_c) * n + q_z + n_blocks).astype(jnp.float32)
    lane = lax.broadcasted_iota(jnp.int32, (n_pass, 128), 1)
    slots = jnp.zeros((n_pass, 128), jnp.float32)
    for k in range(SLOTS):
        mine = rank == float(k)
        slots = jnp.where(
            lane == k, jnp.sum(jnp.where(mine, at_a, 0.0), axis=1, keepdims=True), slots
        )
        slots = jnp.where(
            lane == SLOTS + k, jnp.sum(jnp.where(mine, at_b, 0.0), axis=1, keepdims=True), slots
        )
    slot_vec[...] = slots.astype(jnp.int32)
    to_smem = pltpu.make_async_copy(slot_vec, slot_smem, local_sem.at[3])
    to_smem.start()

    take_quarter(nx - 1)

    def fetch(p):
        for u in range(pass_len):
            fetched[pl.ds(p * pass_len + u, 1)] = book32[pl.ds(id_ref[p, u], 1)]

    loop(0, n_pass, fetch)

    def decode(p):
        span = pl.ds(pl.multiple_of(p * pass_len, pass_len), pass_len)
        emb[span] = (fetched[span] + extra32[p]).astype(jnp.bfloat16)

    loop(0, n_pass, decode)

    def last_quarter(h):
        r = near(rep, nx - 1, nx)
        for t in range(n):
            tile = h * n + t
            best_acc[tile] = jnp.maximum(best_acc[tile], best_of(tile, r))

    loop(0, 2, last_quarter)
    to_smem.wait()

    slot_iota = lax.broadcasted_iota(jnp.int32, (pass_len, SLOTS * 2 * HALF), 0)

    def score(i):
        for u in range(4):
            p = i * 4 + u
            parts = []
            for k in range(SLOTS):
                parts.append(toks[jnp.clip(slot_smem[p, k], 0, n_blocks - 1)])
                parts.append(
                    toks[jnp.clip(slot_smem[p, SLOTS + k], n_blocks, 2 * n_blocks - 1)]
                )
            picked = jnp.concatenate(parts, axis=0)
            span = pl.ds(pl.multiple_of(p * pass_len, pass_len), pass_len)
            similar = lax.dot_general(
                emb[span], picked, DIMS, preferred_element_type=jnp.float32
            )
            similar = jnp.where(slot_iota < length_ref[p], similar, FAR_BELOW)
            pair_best[pl.ds(p, 1)] = jnp.max(similar, axis=0, keepdims=True)

    loop(0, n_pass // 4, score)

    tok_of = lax.broadcasted_iota(jnp.int32, (SLOTS * 2 * HALF, 128), 0) >> 5
    col_of = lax.broadcasted_iota(jnp.int32, (SLOTS * 2 * HALF, 128), 1)
    ones = (tok_of == col_of).astype(jnp.float32)
    slot_score = jnp.dot(
        pair_best[...], ones, preferred_element_type=jnp.float32,
        precision=lax.Precision.HIGHEST,
    )
    table = jnp.zeros((n_pass, n_query), jnp.float32)
    for k in range(SLOTS):
        table = jnp.where(rank == float(k), slot_score[:, k : k + 1], table)
    chosen = jnp.full((n_cand, n_query), FAR_BELOW, jnp.float32)
    for p in range(n_pass):
        chosen = jnp.where(cand_t == first_pass + p, table[p : p + 1, :], chosen)
    chosen = jnp.transpose(
        jnp.concatenate([chosen, jnp.full((128 - n_cand, n_query), FAR_BELOW, jnp.float32)], axis=0)
    )

    best = jnp.max(best_acc[...], axis=1)
    row_of = lax.broadcasted_iota(jnp.int32, (n, 128), 0)
    lane_of = lax.broadcasted_iota(jnp.int32, (n, 128), 1)
    in_a = (lane_of >= n_cand) & (lane_of < n_cand + HALF)
    in_b = (lane_of >= n_cand + HALF) & (lane_of < n_cand + 2 * HALF)

    def fit(part):
        if lane_half == 128:
            return part
        return jnp.concatenate([part, jnp.full((n, 128 - lane_half), FAR_BELOW, jnp.float32)], axis=1)

    for c_ in range(CORES):
        cols = slice(c_ * lane_half, (c_ + 1) * lane_half)
        best_a = fit(best[0:n, cols])
        best_b = fit(best[n : 2 * n, cols])
        for y_ in range(n):
            shift = (n_cand - y_ * HALF) % 128
            part_a = pltpu.roll(best_a, shift, 1) if shift else best_a
            part_b = jnp.where(
                (lane_of >> 4) == row_of, jnp.broadcast_to(best_b[y_ : y_ + 1], (n, 128)), FAR_BELOW
            )
            for step in (64, 32, 16):
                part_b = jnp.maximum(part_b, pltpu.roll(part_b, step, 1))
            t = c_ * n + y_
            tile = chosen[t * n : (t + 1) * n]
            tiles[t] = jnp.where(in_a, part_a, jnp.where(in_b, part_b, tile))

    me = c * n + y

    def merge1_copy(k, c_):
        ty = near(y, k, n)
        return rcopy(
            tiles.at[c_ * n + ty], got1.at[me], sx.at[c_ * n + ty], rx.at[me], at(z, ty, c_)
        )

    def merge1_start(k):
        merge1_copy(k, c).start()
        merge1_copy(k, 1 - c).start()

    loop(1, n, merge1_start)
    merge1_copy(0, 1 - c).start()

    def from1(k, c_):
        t = c_ * n + near(y, k, n)
        rcopy(tiles.at[t], got1.at[t], sx.at[t], rx.at[t], sibling).wait_recv()
        return got1[t]

    merged = lax.fori_loop(
        1, n,
        lambda k, acc: jnp.maximum(acc, jnp.maximum(from1(k, c), from1(k, 1 - c))),
        tiles[me],
    )
    merged = jnp.maximum(merged, from1(0, 1 - c))
    line[...] = merged

    def merge2_copy(k):
        tz = near(z, k, n)
        return rcopy(line.at[pl.ds(tz, 1)], got2.at[pl.ds(z, 1)], sy.at[k], ry.at[z], at(tz, y, c))

    loop(1, n, lambda k: merge2_copy(k).start())

    def from2(k, acc):
        tz = near(z, k, n)
        row = got2.at[pl.ds(tz, 1)]
        rcopy(row, row, sy.at[k], ry.at[tz], sibling).wait_recv()
        return jnp.maximum(acc, got2[pl.ds(tz, 1)])

    final = lax.fori_loop(1, n, from2, line[pl.ds(z, 1)])
    score_out[...] = final[:, 0:n_cand]
    best_out[...] = pltpu.roll(final, 128 - n_cand, 1)[:, 0 : 2 * HALF]

    def sent(k):
        for copy in hop1_copies(k) + hop2_copies(k):
            copy.wait_send()
        pass_on(k, 0).wait_send()
        pass_on(k, 1).wait_send()
        merge1_copy(k, c).wait_send()
        merge1_copy(k, 1 - c).wait_send()
        merge2_copy(k).wait_send()

    loop(1, n, sent)
    loop(1, nx, lambda k: book_copy(k).wait_send())
    pass_on(0, 0).wait_send()
    pass_on(0, 1).wait_send()
    hand_cands.wait_send()
    merge1_copy(0, 1 - c).wait_send()


def on_device(
    queries, candidates, codebook, bucket_weights, centroid_ids, residual_codes, passage_lengths, sizes
):
    n, nx = sizes
    query_len, width = queries.shape[2:]
    n_cand = candidates.shape[2]
    quarter = codebook.shape[0]
    n_pass, pass_len = centroid_ids.shape
    n_query = CORES * n * n
    tile_width = CORES * n * HALF
    vmem = pl.BlockSpec(memory_space=pltpu.VMEM)
    hbm = pl.BlockSpec(memory_space=pltpu.HBM)
    dma = pltpu.SemaphoreType.DMA
    f32, bf16, i32 = jnp.float32, jnp.bfloat16, jnp.int32
    best, scores = pl.pallas_call(
        functools.partial(kernel, n, nx),
        out_shape=(
            jax.ShapeDtypeStruct((1, query_len), f32),
            jax.ShapeDtypeStruct((1, n_cand), f32),
        ),
        in_specs=[hbm] * 7,
        out_specs=(vmem, vmem),
        scratch_shapes=[
            pltpu.VMEM((query_len, width), bf16),
            pltpu.VMEM((1, n_cand), i32),
            pltpu.SMEM(bucket_weights.shape, f32),
            pltpu.SMEM(passage_lengths.shape, i32),
            pltpu.SMEM(centroid_ids.shape, i32),
            pltpu.VMEM((nx * quarter, width), bf16),
            pltpu.VMEM((nx * quarter, width), f32),
            pltpu.VMEM((2 * n_query, HALF, width), bf16),
            pltpu.VMEM(residual_codes.shape, i32),
            pltpu.VMEM(residual_codes.shape, f32),
            pltpu.VMEM((n_pass * pass_len, width), f32),
            pltpu.VMEM((n_pass * pass_len, width), bf16),
            pltpu.VMEM((2 * n, 8, tile_width), f32),
            pltpu.VMEM((n_pass, SLOTS * 2 * HALF), f32),
            pltpu.VMEM((1, 128), i32),
            pltpu.VMEM((n, 1, 128), i32),
            pltpu.VMEM((CORES * n, n, 128), i32),
            pltpu.VMEM((n_pass, n_query), f32),
            pltpu.VMEM((n_pass, 128), i32),
            pltpu.SMEM((n_pass, 128), i32),
            pltpu.VMEM((CORES * n, n, 128), f32),
            pltpu.VMEM((CORES * n, n, 128), f32),
            pltpu.VMEM((n, 128), f32),
            pltpu.VMEM((n, 128), f32),
            dma((9,)),
            dma((2, n)), dma((2, n)),
            dma((2, n)), dma((2, n)),
            dma((2, n)), dma((2, n)),
            dma((n,)), dma((n,)),
            dma((n,)), dma((n,)),
            dma((1,)), dma((1,)),
            dma((nx,)), dma((nx,)),
            dma((CORES * n,)), dma((CORES * n,)),
            dma((n,)), dma((n,)),
        ],
        compiler_params=pltpu.CompilerParams(
            collective_id=0, has_side_effects=True, vmem_limit_bytes=60 << 20
        ),
        cost_estimate=pl.CostEstimate(flops=4 << 30, bytes_accessed=2 << 20, transcendentals=0),
        name="late_interaction",
    )(
        queries.reshape(query_len, width), candidates.reshape(1, n_cand), bucket_weights,
        passage_lengths, centroid_ids, codebook, residual_codes,
    )
    return best.reshape(1, 1, query_len), scores.reshape(1, 1, n_cand)


def solution(mesh):
    from jax.sharding import PartitionSpec as P

    nx = mesh.shape["rep"]
    n = math.isqrt(mesh.shape["shard"] // CORES)
    in_specs = (
        P("rep", "shard", None, None),
        P("rep", "shard", None),
        P(("shard", "rep"), None),
        P(),
        P("shard", None),
        P("shard", None, None),
        P("shard"),
    )
    out_specs = (P("rep", "shard", None), P("rep", "shard", None))
    return jax.shard_map(
        functools.partial(on_device, sizes=(n, nx)),
        mesh=mesh, in_specs=in_specs, out_specs=out_specs, check_vma=False,
    )
```

```python
import functools
import math

import jax
import jax.numpy as jnp
from jax import lax
from jax.experimental import pallas as pl
from jax.experimental.pallas import tpu as pltpu

FAR_BELOW = -1e30
MESH = pl.DeviceIdType.MESH
CORES = 2
SLOTS = 8
HALF = 16
DIMS = (((1,), (1,)), ((), ()))


def kernel(
    n, nx, query_hbm, cand_hbm, weight_hbm, length_hbm, id_hbm, book_hbm, code_hbm,
    row_out,
    query_ref, cand_ref, weight_ref, length_ref, id_ref,
    book, book32, toks, codes, extra32, fetched, emb, best_acc, pair_best,
    cand_row, cand_line, cand_all, hits, slot_vec, slot_smem, tiles, got1, line, got2,
    local_sem, s1, r1, s2, r2, s3, r3, sc1, rc1, sc2, rc2, sc3, rc3, sb, rb, sx, rx, sy, ry,
):
    quarter = book_hbm.shape[0]
    n_pass, pass_len = id_ref.shape
    n_cand = cand_ref.shape[1]
    side = CORES * n
    n_blocks = n * side
    n_query = CORES * n * n
    width = side * HALF
    lane_half = n * HALF

    shard = lax.axis_index("shard")
    rep = lax.axis_index("rep")
    c = lax.rem(shard, CORES)
    y = lax.rem(shard // CORES, n)
    z = shard // (CORES * n)

    def at(z_, y_, c_):
        return {"shard": (z_ * n + y_) * CORES + c_, "rep": rep}

    def near(me, k, count):
        step = (k + 1) // 2
        return lax.rem(jnp.where(lax.rem(k, 2) == 1, me + step, me + count - step), count)

    def rcopy(src, dst, send, recv, dev):
        return pltpu.make_async_remote_copy(
            src_ref=src, dst_ref=dst, send_sem=send, recv_sem=recv,
            device_id=dev, device_id_type=MESH,
        )

    sibling = at(z, y, 1 - c)

    def loop(low, high, body):
        def step(k, carry):
            body(k)
            return carry
        lax.fori_loop(low, high, step, 0)

    def blocks_a(z_, c_):
        return toks.at[pl.ds((z_ * CORES + c_) * n, n)]

    def blocks_b(y_, c_):
        return toks.at[pl.ds(n_blocks + (y_ * CORES + c_) * n, n)]

    own_rows = pl.ds(pl.multiple_of(rep * quarter, quarter), quarter)
    load_book = pltpu.make_async_copy(book_hbm, book.at[own_rows], local_sem.at[0])
    load_codes = pltpu.make_async_copy(code_hbm, codes, local_sem.at[1])
    small = [
        pltpu.make_async_copy(source, target, local_sem.at[4 + i])
        for i, (source, target) in enumerate((
            (query_hbm, query_ref), (cand_hbm, cand_ref), (weight_hbm, weight_ref),
            (length_hbm, length_ref), (id_hbm, id_ref),
        ))
    ]
    for copy in small:
        copy.start()
    load_book.start()
    load_codes.start()

    barrier = pltpu.get_barrier_semaphore()

    def greet(dev):
        pl.semaphore_signal(barrier, inc=1, device_id=dev, device_id_type=MESH)

    def greet_line(k):
        greet(at(z, near(y, k, n), c))
        greet(at(z, near(y, k, n), 1 - c))
        greet(at(near(z, k, n), y, c))

    loop(1, n, greet_line)
    loop(1, nx, lambda k: greet({"shard": shard, "rep": near(rep, k, nx)}))
    greet(sibling)

    for copy in small:
        copy.wait()
    toks[(z * CORES + c) * n + y] = query_ref[0:HALF]
    toks[n_blocks + (y * CORES + c) * n + z] = query_ref[HALF : 2 * HALF]
    cand_row[...] = jnp.full(cand_row.shape, -1, jnp.int32)
    cand_row[:, 0:n_cand] = cand_ref[...]
    cand_line[pl.ds(y, 1)] = cand_row[...].reshape(1, 1, 128)

    pl.semaphore_wait(barrier, 3 * (n - 1) + nx)

    def hop1_copies(k):
        ty, tz = near(y, k, n), near(z, k, n)
        block_a = toks.at[(z * CORES + c) * n + y]
        block_b = toks.at[n_blocks + (y * CORES + c) * n + z]
        return (
            rcopy(cand_line.at[y], cand_line.at[y], sc1.at[k], rc1.at[y], at(z, ty, c)),
            rcopy(block_a, block_a, s1.at[0, k], r1.at[0, y], at(z, ty, c)),
            rcopy(block_b, block_b, s1.at[1, k], r1.at[1, z], at(tz, y, c)),
        )

    def book_copy(k):
        return rcopy(
            book_hbm, book.at[own_rows], sb.at[k], rb.at[rep],
            {"shard": shard, "rep": near(rep, k, nx)},
        )

    def hop1_start(k):
        for copy in hop1_copies(k):
            copy.start()

    loop(1, n, hop1_start)
    loop(1, nx, lambda k: book_copy(k).start())

    load_codes.wait()

    def residual(p):
        part = codes[p]
        value = jnp.zeros(part.shape, jnp.float32)
        for level in range(weight_ref.shape[0]):
            value = jnp.where(part == level, weight_ref[level], value)
        extra32[p] = value

    loop(0, n_pass, residual)

    def hop1_wait(k):
        ty, tz = near(y, k, n), near(z, k, n)
        block_a = toks.at[(z * CORES + c) * n + ty]
        block_b = toks.at[n_blocks + (y * CORES + c) * n + tz]
        rcopy(cand_line.at[ty], cand_line.at[ty], sc1.at[k], rc1.at[ty], sibling).wait_recv()
        rcopy(block_a, block_a, s1.at[0, k], r1.at[0, ty], sibling).wait_recv()
        rcopy(block_b, block_b, s1.at[1, k], r1.at[1, tz], sibling).wait_recv()

    loop(1, n, hop1_wait)

    def cand_slab(z_, c_):
        return cand_all.at[pl.ds(c_ * n, n), pl.ds(z_, 1)]

    def hop2_copies(k):
        ty, tz = near(y, k, n), near(z, k, n)
        return (
            rcopy(blocks_a(z, c), blocks_a(z, c), s2.at[0, k], r2.at[0, z], at(tz, y, c)),
            rcopy(blocks_b(y, c), blocks_b(y, c), s2.at[1, k], r2.at[1, y], at(z, ty, c)),
            rcopy(cand_line, cand_slab(z, c), sc2.at[k], rc2.at[z], at(tz, y, c)),
        )

    def hop2_start(k):
        for copy in hop2_copies(k):
            copy.start()

    loop(1, n, hop2_start)
    own_cands = pltpu.make_async_copy(cand_line, cand_slab(z, c), local_sem.at[2])
    own_cands.start()

    def pass_on(k, half):
        if half == 0:
            zk = near(z, k, n)
            return rcopy(blocks_a(zk, c), blocks_a(zk, c), s3.at[0, k], r3.at[0, zk], sibling)
        yk = near(y, k, n)
        return rcopy(blocks_b(yk, c), blocks_b(yk, c), s3.at[1, k], r3.at[1, yk], sibling)

    pass_on(0, 0).start()
    pass_on(0, 1).start()
    own_cands.wait()

    def span_of(r):
        return pl.ds(pl.multiple_of(r * quarter, quarter), quarter)

    def best_of(tile, r):
        token = toks[pl.ds(tile * side, side)].reshape(width, toks.shape[2])
        scored = lax.dot_general(book[span_of(r)], token, DIMS, preferred_element_type=jnp.float32)
        return jnp.max(scored.reshape(quarter // 8, 8, width), axis=0)

    def widen(r):
        book32[span_of(r)] = book[span_of(r)].astype(jnp.float32)

    def take_quarter(k):
        r = near(rep, k, nx)
        span = book.at[span_of(r)]
        rcopy(book_hbm, span, sb.at[k], rb.at[r], sibling).wait_recv()
        widen(r)

    def pair(k):
        zk, yk = near(z, k, n), near(y, k, n)
        other_a, other_b = blocks_a(zk, 1 - c), blocks_b(yk, 1 - c)
        rcopy(other_a, other_a, s3.at[0, k], r3.at[0, zk], sibling).wait_recv()
        rcopy(other_b, other_b, s3.at[1, k], r3.at[1, yk], sibling).wait_recv()
        for tile in (zk, n + yk):
            top = best_of(tile, rep)
            for j in range(1, nx - 1):
                top = jnp.maximum(top, best_of(tile, near(rep, j, nx)))
            best_acc[tile] = top

    def forward(k):
        zk, yk = near(z, k, n), near(y, k, n)
        rcopy(blocks_a(zk, c), blocks_a(zk, c), s2.at[0, k], r2.at[0, zk], sibling).wait_recv()
        pass_on(k, 0).start()
        rcopy(blocks_b(yk, c), blocks_b(yk, c), s2.at[1, k], r2.at[1, yk], sibling).wait_recv()
        pass_on(k, 1).start()

    load_book.wait()
    widen(rep)
    loop(1, nx - 1, take_quarter)
    pair(0)
    forward(1)

    if n > 2:
        forward(2)

    def arrive(k):
        forward(k)
        pair(k - 2)

    loop(3, n, arrive)

    def cands_wait(k):
        zk = near(z, k, n)
        rcopy(cand_line, cand_slab(zk, c), sc2.at[k], rc2.at[zk], sibling).wait_recv()

    loop(1, n, cands_wait)

    def cand_core(c_):
        return cand_all.at[pl.ds(c_ * n, n)]

    hand_cands = rcopy(cand_core(c), cand_core(c), sc3.at[0], rc3.at[0], sibling)
    hand_cands.start()
    loop(max(1, n - 2), n, pair)

    rcopy(cand_core(1 - c), cand_core(1 - c), sc3.at[0], rc3.at[0], sibling).wait_recv()
    cand_t = jnp.transpose(cand_all[...].reshape(n_query, 128))[0:n_cand]
    first_pass = shard * n_pass
    for p in range(n_pass):
        hits[p : p + 1, :] = jnp.max(
            jnp.where(cand_t == first_pass + p, 1.0, 0.0), axis=0, keepdims=True
        )
    hit = hits[...]
    before = (
        lax.broadcasted_iota(jnp.int32, (n_query, n_query), 0)
        < lax.broadcasted_iota(jnp.int32, (n_query, n_query), 1)
    ).astype(jnp.bfloat16)
    rank = jnp.dot(hit.astype(jnp.bfloat16), before, preferred_element_type=jnp.float32)
    rank = jnp.where(hit > 0.5, rank, -1.0)
    bits = n.bit_length() - 1
    q_index = lax.broadcasted_iota(jnp.int32, (n_pass, n_query), 1)
    q_z = q_index & (n - 1)
    q_y = (q_index >> bits) & (n - 1)
    q_c = q_index >> (2 * bits)
    at_a = ((q_z * CORES + q_c) * n + q_y).astype(jnp.float32)
    at_b = ((q_y * CORES + q_c) * n + q_z + n_blocks).astype(jnp.float32)
    lane = lax.broadcasted_iota(jnp.int32, (n_pass, 128), 1)
    slots = jnp.zeros((n_pass, 128), jnp.float32)
    for k in range(SLOTS):
        mine = rank == float(k)
        slots = jnp.where(
            lane == k, jnp.sum(jnp.where(mine, at_a, 0.0), axis=1, keepdims=True), slots
        )
        slots = jnp.where(
            lane == SLOTS + k, jnp.sum(jnp.where(mine, at_b, 0.0), axis=1, keepdims=True), slots
        )
    slot_vec[...] = slots.astype(jnp.int32)
    to_smem = pltpu.make_async_copy(slot_vec, slot_smem, local_sem.at[3])
    to_smem.start()

    take_quarter(nx - 1)

    def fetch(p):
        for u in range(pass_len):
            fetched[pl.ds(p * pass_len + u, 1)] = book32[pl.ds(id_ref[p, u], 1)]

    loop(0, n_pass, fetch)

    def decode(p):
        span = pl.ds(pl.multiple_of(p * pass_len, pass_len), pass_len)
        emb[span] = (fetched[span] + extra32[p]).astype(jnp.bfloat16)

    loop(0, n_pass, decode)

    def last_quarter(h):
        r = near(rep, nx - 1, nx)
        for t in range(n):
            tile = h * n + t
            best_acc[tile] = jnp.maximum(best_acc[tile], best_of(tile, r))

    loop(0, 2, last_quarter)
    to_smem.wait()

    slot_iota = lax.broadcasted_iota(jnp.int32, (pass_len, SLOTS * 2 * HALF), 0)

    def score(i):
        for u in range(4):
            p = i * 4 + u
            parts = []
            for k in range(SLOTS):
                parts.append(toks[jnp.clip(slot_smem[p, k], 0, n_blocks - 1)])
                parts.append(
                    toks[jnp.clip(slot_smem[p, SLOTS + k], n_blocks, 2 * n_blocks - 1)]
                )
            picked = jnp.concatenate(parts, axis=0)
            span = pl.ds(pl.multiple_of(p * pass_len, pass_len), pass_len)
            similar = lax.dot_general(
                emb[span], picked, DIMS, preferred_element_type=jnp.float32
            )
            similar = jnp.where(slot_iota < length_ref[p], similar, FAR_BELOW)
            pair_best[pl.ds(p, 1)] = jnp.max(similar, axis=0, keepdims=True)

    loop(0, n_pass // 4, score)

    tok_of = lax.broadcasted_iota(jnp.int32, (SLOTS * 2 * HALF, 128), 0) >> 5
    col_of = lax.broadcasted_iota(jnp.int32, (SLOTS * 2 * HALF, 128), 1)
    ones = (tok_of == col_of).astype(jnp.float32)
    slot_score = jnp.dot(
        pair_best[...], ones, preferred_element_type=jnp.float32,
        precision=lax.Precision.HIGHEST,
    )
    table = jnp.zeros((n_pass, n_query), jnp.float32)
    for k in range(SLOTS):
        table = jnp.where(rank == float(k), slot_score[:, k : k + 1], table)
    chosen = jnp.full((n_cand, n_query), FAR_BELOW, jnp.float32)
    for p in range(n_pass):
        chosen = jnp.where(cand_t == first_pass + p, table[p : p + 1, :], chosen)
    chosen = jnp.transpose(
        jnp.concatenate([chosen, jnp.full((128 - n_cand, n_query), FAR_BELOW, jnp.float32)], axis=0)
    )

    best = jnp.max(best_acc[...], axis=1)
    row_of = lax.broadcasted_iota(jnp.int32, (n, 128), 0)
    lane_of = lax.broadcasted_iota(jnp.int32, (n, 128), 1)
    in_a = (lane_of >= n_cand) & (lane_of < n_cand + HALF)
    in_b = (lane_of >= n_cand + HALF) & (lane_of < n_cand + 2 * HALF)

    def fit(part):
        if lane_half == 128:
            return part
        return jnp.concatenate([part, jnp.full((n, 128 - lane_half), FAR_BELOW, jnp.float32)], axis=1)

    for c_ in range(CORES):
        cols = slice(c_ * lane_half, (c_ + 1) * lane_half)
        best_a = fit(best[0:n, cols])
        best_b = fit(best[n : 2 * n, cols])
        for y_ in range(n):
            shift = (n_cand - y_ * HALF) % 128
            part_a = pltpu.roll(best_a, shift, 1) if shift else best_a
            part_b = jnp.where(
                (lane_of >> 4) == row_of, jnp.broadcast_to(best_b[y_ : y_ + 1], (n, 128)), FAR_BELOW
            )
            for step in (64, 32, 16):
                part_b = jnp.maximum(part_b, pltpu.roll(part_b, step, 1))
            t = c_ * n + y_
            tile = chosen[t * n : (t + 1) * n]
            tiles[t] = jnp.where(in_a, part_a, jnp.where(in_b, part_b, tile))

    me = c * n + y

    def merge1_copy(k, c_):
        ty = near(y, k, n)
        return rcopy(
            tiles.at[c_ * n + ty], got1.at[me], sx.at[c_ * n + ty], rx.at[me], at(z, ty, c_)
        )

    def merge1_start(k):
        merge1_copy(k, c).start()
        merge1_copy(k, 1 - c).start()

    loop(1, n, merge1_start)
    merge1_copy(0, 1 - c).start()

    def gathered(k):
        for copy in hop1_copies(k) + hop2_copies(k):
            copy.wait_send()
        pass_on(k, 0).wait_send()
        pass_on(k, 1).wait_send()

    loop(1, n, gathered)
    loop(1, nx, lambda k: book_copy(k).wait_send())
    pass_on(0, 0).wait_send()
    pass_on(0, 1).wait_send()
    hand_cands.wait_send()

    def from1(k, c_):
        t = c_ * n + near(y, k, n)
        rcopy(tiles.at[t], got1.at[t], sx.at[t], rx.at[t], sibling).wait_recv()
        return got1[t]

    merged = lax.fori_loop(
        1, n,
        lambda k, acc: jnp.maximum(acc, jnp.maximum(from1(k, c), from1(k, 1 - c))),
        tiles[me],
    )
    merged = jnp.maximum(merged, from1(0, 1 - c))
    line[...] = merged

    def merge2_copy(k):
        tz = near(z, k, n)
        return rcopy(line.at[pl.ds(tz, 1)], got2.at[pl.ds(z, 1)], sy.at[k], ry.at[z], at(tz, y, c))

    loop(1, n, lambda k: merge2_copy(k).start())

    def merge1_sent(k):
        merge1_copy(k, c).wait_send()
        merge1_copy(k, 1 - c).wait_send()

    loop(1, n, merge1_sent)
    merge1_copy(0, 1 - c).wait_send()

    def from2(k, acc):
        tz = near(z, k, n)
        row = got2.at[pl.ds(tz, 1)]
        rcopy(row, row, sy.at[k], ry.at[tz], sibling).wait_recv()
        return jnp.maximum(acc, got2[pl.ds(tz, 1)])

    final = lax.fori_loop(1, n, from2, line[pl.ds(z, 1)])
    row_out[...] = final
    loop(1, n, lambda k: merge2_copy(k).wait_send())


def on_device(
    queries, candidates, codebook, bucket_weights, centroid_ids, residual_codes, passage_lengths, sizes
):
    n, nx = sizes
    query_len, width = queries.shape[2:]
    n_cand = candidates.shape[2]
    quarter = codebook.shape[0]
    n_pass, pass_len = centroid_ids.shape
    n_query = CORES * n * n
    tile_width = CORES * n * HALF
    vmem = pl.BlockSpec(memory_space=pltpu.VMEM)
    hbm = pl.BlockSpec(memory_space=pltpu.HBM)
    dma = pltpu.SemaphoreType.DMA
    f32, bf16, i32 = jnp.float32, jnp.bfloat16, jnp.int32
    row = pl.pallas_call(
        functools.partial(kernel, n, nx),
        out_shape=jax.ShapeDtypeStruct((1, 128), f32),
        in_specs=[hbm] * 7,
        out_specs=vmem,
        scratch_shapes=[
            pltpu.VMEM((query_len, width), bf16),
            pltpu.VMEM((1, n_cand), i32),
            pltpu.SMEM(bucket_weights.shape, f32),
            pltpu.SMEM(passage_lengths.shape, i32),
            pltpu.SMEM(centroid_ids.shape, i32),
            pltpu.VMEM((nx * quarter, width), bf16),
            pltpu.VMEM((nx * quarter, width), f32),
            pltpu.VMEM((2 * n_query, HALF, width), bf16),
            pltpu.VMEM(residual_codes.shape, i32),
            pltpu.VMEM(residual_codes.shape, f32),
            pltpu.VMEM((n_pass * pass_len, width), f32),
            pltpu.VMEM((n_pass * pass_len, width), bf16),
            pltpu.VMEM((2 * n, 8, tile_width), f32),
            pltpu.VMEM((n_pass, SLOTS * 2 * HALF), f32),
            pltpu.VMEM((1, 128), i32),
            pltpu.VMEM((n, 1, 128), i32),
            pltpu.VMEM((CORES * n, n, 128), i32),
            pltpu.VMEM((n_pass, n_query), f32),
            pltpu.VMEM((n_pass, 128), i32),
            pltpu.SMEM((n_pass, 128), i32),
            pltpu.VMEM((CORES * n, n, 128), f32),
            pltpu.VMEM((CORES * n, n, 128), f32),
            pltpu.VMEM((n, 128), f32),
            pltpu.VMEM((n, 128), f32),
            dma((9,)),
            dma((2, n)), dma((2, n)),
            dma((2, n)), dma((2, n)),
            dma((2, n)), dma((2, n)),
            dma((n,)), dma((n,)),
            dma((n,)), dma((n,)),
            dma((1,)), dma((1,)),
            dma((nx,)), dma((nx,)),
            dma((CORES * n,)), dma((CORES * n,)),
            dma((n,)), dma((n,)),
        ],
        compiler_params=pltpu.CompilerParams(
            collective_id=0, has_side_effects=True, vmem_limit_bytes=60 << 20
        ),
        cost_estimate=pl.CostEstimate(flops=4 << 30, bytes_accessed=2 << 20, transcendentals=0),
        name="late_interaction",
    )(
        queries.reshape(query_len, width), candidates.reshape(1, n_cand), bucket_weights,
        passage_lengths, centroid_ids, codebook, residual_codes,
    )
    row = row.reshape(1, 1, 128)
    return row[:, :, n_cand : n_cand + query_len], row[:, :, 0:n_cand]


def solution(mesh):
    from jax.sharding import PartitionSpec as P

    nx = mesh.shape["rep"]
    n = math.isqrt(mesh.shape["shard"] // CORES)
    in_specs = (
        P("rep", "shard", None, None),
        P("rep", "shard", None),
        P(("shard", "rep"), None),
        P(),
        P("shard", None),
        P("shard", None, None),
        P("shard"),
    )
    out_specs = (P("rep", "shard", None), P("rep", "shard", None))
    return jax.shard_map(
        functools.partial(on_device, sizes=(n, nx)),
        mesh=mesh, in_specs=in_specs, out_specs=out_specs, check_vma=False,
    )
```

```python
import functools
import math

import jax
import jax.numpy as jnp
from jax import lax
from jax.experimental import pallas as pl
from jax.experimental.pallas import tpu as pltpu

FAR_BELOW = -1e30
MESH = pl.DeviceIdType.MESH
CORES = 2
SLOTS = 8
HALF = 16
DIMS = (((1,), (1,)), ((), ()))


def kernel(
    n, nx, query_hbm, cand_hbm, weight_hbm, length_hbm, id_hbm, book_hbm, code_hbm,
    row_out,
    query_ref, cand_ref, weight_ref, length_ref, id_ref,
    book, book32, toks, codes, extra32, fetched, emb, best_acc, pair_best,
    cand_row, cand_line, cand_all, hits, slot_vec, slot_smem, tiles, got1, line, got2,
    local_sem, s1, r1, s2, r2, s3, r3, sc1, rc1, sc2, rc2, sc3, rc3, sb, rb, sx, rx, sy, ry,
):
    quarter = book_hbm.shape[0]
    n_pass, pass_len = id_ref.shape
    n_cand = cand_ref.shape[1]
    side = CORES * n
    n_blocks = n * side
    n_query = CORES * n * n
    width = side * HALF
    lane_half = n * HALF

    shard = lax.axis_index("shard")
    rep = lax.axis_index("rep")
    c = lax.rem(shard, CORES)
    y = lax.rem(shard // CORES, n)
    z = shard // (CORES * n)

    def at(z_, y_, c_):
        return {"shard": (z_ * n + y_) * CORES + c_, "rep": rep}

    def near(me, k, count):
        step = (k + 1) // 2
        return lax.rem(jnp.where(lax.rem(k, 2) == 1, me + step, me + count - step), count)

    def rcopy(src, dst, send, recv, dev):
        return pltpu.make_async_remote_copy(
            src_ref=src, dst_ref=dst, send_sem=send, recv_sem=recv,
            device_id=dev, device_id_type=MESH,
        )

    sibling = at(z, y, 1 - c)

    def loop(low, high, body):
        def step(k, carry):
            body(k)
            return carry
        lax.fori_loop(low, high, step, 0)

    def blocks_a(z_, c_):
        return toks.at[pl.ds((z_ * CORES + c_) * n, n)]

    def blocks_b(y_, c_):
        return toks.at[pl.ds(n_blocks + (y_ * CORES + c_) * n, n)]

    own_rows = pl.ds(pl.multiple_of(rep * quarter, quarter), quarter)
    load_book = pltpu.make_async_copy(book_hbm, book.at[own_rows], local_sem.at[0])
    load_codes = pltpu.make_async_copy(code_hbm, codes, local_sem.at[1])
    barrier = pltpu.get_barrier_semaphore()

    def greet(dev):
        pl.semaphore_signal(barrier, inc=1, device_id=dev, device_id_type=MESH)

    def greet_line(k):
        greet(at(z, near(y, k, n), c))
        greet(at(z, near(y, k, n), 1 - c))
        greet(at(near(z, k, n), y, c))

    loop(1, n, lambda k: greet_line(n - k))
    loop(1, nx, lambda k: greet({"shard": shard, "rep": near(rep, k, nx)}))
    greet(sibling)

    small = [
        pltpu.make_async_copy(source, target, local_sem.at[4 + i])
        for i, (source, target) in enumerate((
            (query_hbm, query_ref), (cand_hbm, cand_ref), (weight_hbm, weight_ref),
            (length_hbm, length_ref), (id_hbm, id_ref),
        ))
    ]
    for copy in small:
        copy.start()
    load_book.start()
    load_codes.start()
    for copy in small:
        copy.wait()
    toks[(z * CORES + c) * n + y] = query_ref[0:HALF]
    toks[n_blocks + (y * CORES + c) * n + z] = query_ref[HALF : 2 * HALF]
    cand_row[...] = jnp.full(cand_row.shape, -1, jnp.int32)
    cand_row[:, 0:n_cand] = cand_ref[...]
    cand_line[pl.ds(y, 1)] = cand_row[...].reshape(1, 1, 128)

    pl.semaphore_wait(barrier, 3 * (n - 1) + nx)

    def hop1_copies(k):
        ty, tz = near(y, k, n), near(z, k, n)
        block_a = toks.at[(z * CORES + c) * n + y]
        block_b = toks.at[n_blocks + (y * CORES + c) * n + z]
        return (
            rcopy(cand_line.at[y], cand_line.at[y], sc1.at[k], rc1.at[y], at(z, ty, c)),
            rcopy(block_a, block_a, s1.at[0, k], r1.at[0, y], at(z, ty, c)),
            rcopy(block_b, block_b, s1.at[1, k], r1.at[1, z], at(tz, y, c)),
        )

    def book_copy(k):
        return rcopy(
            book_hbm, book.at[own_rows], sb.at[k], rb.at[rep],
            {"shard": shard, "rep": near(rep, k, nx)},
        )

    def hop1_start(k):
        for copy in hop1_copies(k):
            copy.start()

    loop(1, n, lambda k: hop1_start(n - k))
    loop(1, nx, lambda k: book_copy(k).start())

    load_codes.wait()

    def residual(p):
        part = codes[p]
        value = jnp.zeros(part.shape, jnp.float32)
        for level in range(weight_ref.shape[0]):
            value = jnp.where(part == level, weight_ref[level], value)
        extra32[p] = value

    loop(0, n_pass, residual)

    def hop1_wait(k):
        ty, tz = near(y, k, n), near(z, k, n)
        block_a = toks.at[(z * CORES + c) * n + ty]
        block_b = toks.at[n_blocks + (y * CORES + c) * n + tz]
        rcopy(cand_line.at[ty], cand_line.at[ty], sc1.at[k], rc1.at[ty], sibling).wait_recv()
        rcopy(block_a, block_a, s1.at[0, k], r1.at[0, ty], sibling).wait_recv()
        rcopy(block_b, block_b, s1.at[1, k], r1.at[1, tz], sibling).wait_recv()

    loop(1, n, hop1_wait)

    def cand_slab(z_, c_):
        return cand_all.at[pl.ds(c_ * n, n), pl.ds(z_, 1)]

    def hop2_copies(k):
        ty, tz = near(y, k, n), near(z, k, n)
        return (
            rcopy(blocks_a(z, c), blocks_a(z, c), s2.at[0, k], r2.at[0, z], at(tz, y, c)),
            rcopy(blocks_b(y, c), blocks_b(y, c), s2.at[1, k], r2.at[1, y], at(z, ty, c)),
            rcopy(cand_line, cand_slab(z, c), sc2.at[k], rc2.at[z], at(tz, y, c)),
        )

    def hop2_start(k):
        for copy in hop2_copies(k):
            copy.start()

    loop(1, n, hop2_start)
    own_cands = pltpu.make_async_copy(cand_line, cand_slab(z, c), local_sem.at[2])
    own_cands.start()

    def pass_on(k, half):
        if half == 0:
            zk = near(z, k, n)
            return rcopy(blocks_a(zk, c), blocks_a(zk, c), s3.at[0, k], r3.at[0, zk], sibling)
        yk = near(y, k, n)
        return rcopy(blocks_b(yk, c), blocks_b(yk, c), s3.at[1, k], r3.at[1, yk], sibling)

    pass_on(0, 0).start()
    pass_on(0, 1).start()
    own_cands.wait()

    def span_of(r):
        return pl.ds(pl.multiple_of(r * quarter, quarter), quarter)

    def best_of(tile, r):
        token = toks[pl.ds(tile * side, side)].reshape(width, toks.shape[2])
        scored = lax.dot_general(book[span_of(r)], token, DIMS, preferred_element_type=jnp.float32)
        return jnp.max(scored.reshape(quarter // 8, 8, width), axis=0)

    def widen(r):
        book32[span_of(r)] = book[span_of(r)].astype(jnp.float32)

    def take_quarter(k):
        r = near(rep, k, nx)
        span = book.at[span_of(r)]
        rcopy(book_hbm, span, sb.at[k], rb.at[r], sibling).wait_recv()
        widen(r)

    def pair(k):
        zk, yk = near(z, k, n), near(y, k, n)
        other_a, other_b = blocks_a(zk, 1 - c), blocks_b(yk, 1 - c)
        rcopy(other_a, other_a, s3.at[0, k], r3.at[0, zk], sibling).wait_recv()
        rcopy(other_b, other_b, s3.at[1, k], r3.at[1, yk], sibling).wait_recv()
        for tile in (zk, n + yk):
            top = best_of(tile, rep)
            for j in range(1, nx - 1):
                top = jnp.maximum(top, best_of(tile, near(rep, j, nx)))
            best_acc[tile] = top

    def forward(k):
        zk, yk = near(z, k, n), near(y, k, n)
        rcopy(blocks_a(zk, c), blocks_a(zk, c), s2.at[0, k], r2.at[0, zk], sibling).wait_recv()
        pass_on(k, 0).start()
        rcopy(blocks_b(yk, c), blocks_b(yk, c), s2.at[1, k], r2.at[1, yk], sibling).wait_recv()
        pass_on(k, 1).start()

    load_book.wait()
    widen(rep)
    loop(1, nx - 1, take_quarter)
    pair(0)
    forward(1)

    if n > 2:
        forward(2)

    def arrive(k):
        forward(k)
        pair(k - 2)

    loop(3, n, arrive)

    def cands_wait(k):
        zk = near(z, k, n)
        rcopy(cand_line, cand_slab(zk, c), sc2.at[k], rc2.at[zk], sibling).wait_recv()

    loop(1, n, cands_wait)

    def cand_core(c_):
        return cand_all.at[pl.ds(c_ * n, n)]

    hand_cands = rcopy(cand_core(c), cand_core(c), sc3.at[0], rc3.at[0], sibling)
    hand_cands.start()
    loop(max(1, n - 2), n, pair)

    rcopy(cand_core(1 - c), cand_core(1 - c), sc3.at[0], rc3.at[0], sibling).wait_recv()
    cand_t = jnp.transpose(cand_all[...].reshape(n_query, 128))[0:n_cand]
    first_pass = shard * n_pass
    for p in range(n_pass):
        hits[p : p + 1, :] = jnp.max(
            jnp.where(cand_t == first_pass + p, 1.0, 0.0), axis=0, keepdims=True
        )
    hit = hits[...]
    before = (
        lax.broadcasted_iota(jnp.int32, (n_query, n_query), 0)
        < lax.broadcasted_iota(jnp.int32, (n_query, n_query), 1)
    ).astype(jnp.bfloat16)
    rank = jnp.dot(hit.astype(jnp.bfloat16), before, preferred_element_type=jnp.float32)
    rank = jnp.where(hit > 0.5, rank, -1.0)
    bits = n.bit_length() - 1
    q_index = lax.broadcasted_iota(jnp.int32, (n_pass, n_query), 1)
    q_z = q_index & (n - 1)
    q_y = (q_index >> bits) & (n - 1)
    q_c = q_index >> (2 * bits)
    at_a = ((q_z * CORES + q_c) * n + q_y).astype(jnp.float32)
    at_b = ((q_y * CORES + q_c) * n + q_z + n_blocks).astype(jnp.float32)
    lane = lax.broadcasted_iota(jnp.int32, (n_pass, 128), 1)
    slots = jnp.zeros((n_pass, 128), jnp.float32)
    for k in range(SLOTS):
        mine = rank == float(k)
        slots = jnp.where(
            lane == k, jnp.sum(jnp.where(mine, at_a, 0.0), axis=1, keepdims=True), slots
        )
        slots = jnp.where(
            lane == SLOTS + k, jnp.sum(jnp.where(mine, at_b, 0.0), axis=1, keepdims=True), slots
        )
    slot_vec[...] = slots.astype(jnp.int32)
    to_smem = pltpu.make_async_copy(slot_vec, slot_smem, local_sem.at[3])
    to_smem.start()

    take_quarter(nx - 1)

    def fetch(p):
        for u in range(pass_len):
            fetched[pl.ds(p * pass_len + u, 1)] = book32[pl.ds(id_ref[p, u], 1)]

    loop(0, n_pass, fetch)

    def decode(p):
        span = pl.ds(pl.multiple_of(p * pass_len, pass_len), pass_len)
        emb[span] = (fetched[span] + extra32[p]).astype(jnp.bfloat16)

    loop(0, n_pass, decode)

    def last_quarter(h):
        r = near(rep, nx - 1, nx)
        for t in range(n):
            tile = h * n + t
            best_acc[tile] = jnp.maximum(best_acc[tile], best_of(tile, r))

    loop(0, 2, last_quarter)
    to_smem.wait()

    slot_iota = lax.broadcasted_iota(jnp.int32, (pass_len, SLOTS * 2 * HALF), 0)

    def score(i):
        for u in range(4):
            p = i * 4 + u
            parts = []
            for k in range(SLOTS):
                parts.append(toks[jnp.clip(slot_smem[p, k], 0, n_blocks - 1)])
                parts.append(
                    toks[jnp.clip(slot_smem[p, SLOTS + k], n_blocks, 2 * n_blocks - 1)]
                )
            picked = jnp.concatenate(parts, axis=0)
            span = pl.ds(pl.multiple_of(p * pass_len, pass_len), pass_len)
            similar = lax.dot_general(
                emb[span], picked, DIMS, preferred_element_type=jnp.float32
            )
            similar = jnp.where(slot_iota < length_ref[p], similar, FAR_BELOW)
            pair_best[pl.ds(p, 1)] = jnp.max(similar, axis=0, keepdims=True)

    loop(0, n_pass // 4, score)

    tok_of = lax.broadcasted_iota(jnp.int32, (SLOTS * 2 * HALF, 128), 0) >> 5
    col_of = lax.broadcasted_iota(jnp.int32, (SLOTS * 2 * HALF, 128), 1)
    ones = (tok_of == col_of).astype(jnp.float32)
    slot_score = jnp.dot(
        pair_best[...], ones, preferred_element_type=jnp.float32,
        precision=lax.Precision.HIGHEST,
    )
    table = jnp.zeros((n_pass, n_query), jnp.float32)
    for k in range(SLOTS):
        table = jnp.where(rank == float(k), slot_score[:, k : k + 1], table)
    chosen = jnp.full((n_cand, n_query), FAR_BELOW, jnp.float32)
    for p in range(n_pass):
        chosen = jnp.where(cand_t == first_pass + p, table[p : p + 1, :], chosen)
    chosen = jnp.transpose(
        jnp.concatenate([chosen, jnp.full((128 - n_cand, n_query), FAR_BELOW, jnp.float32)], axis=0)
    )

    best = jnp.max(best_acc[...], axis=1)
    row_of = lax.broadcasted_iota(jnp.int32, (n, 128), 0)
    lane_of = lax.broadcasted_iota(jnp.int32, (n, 128), 1)
    in_a = (lane_of >= n_cand) & (lane_of < n_cand + HALF)
    in_b = (lane_of >= n_cand + HALF) & (lane_of < n_cand + 2 * HALF)

    def fit(part):
        if lane_half == 128:
            return part
        return jnp.concatenate([part, jnp.full((n, 128 - lane_half), FAR_BELOW, jnp.float32)], axis=1)

    for c_ in range(CORES):
        cols = slice(c_ * lane_half, (c_ + 1) * lane_half)
        best_a = fit(best[0:n, cols])
        best_b = fit(best[n : 2 * n, cols])
        for y_ in range(n):
            shift = (n_cand - y_ * HALF) % 128
            part_a = pltpu.roll(best_a, shift, 1) if shift else best_a
            part_b = jnp.where(
                (lane_of >> 4) == row_of, jnp.broadcast_to(best_b[y_ : y_ + 1], (n, 128)), FAR_BELOW
            )
            for step in (64, 32, 16):
                part_b = jnp.maximum(part_b, pltpu.roll(part_b, step, 1))
            t = c_ * n + y_
            tile = chosen[t * n : (t + 1) * n]
            tiles[t] = jnp.where(in_a, part_a, jnp.where(in_b, part_b, tile))

    me = c * n + y

    def merge1_copy(k, c_):
        ty = near(y, k, n)
        return rcopy(
            tiles.at[c_ * n + ty], got1.at[me], sx.at[c_ * n + ty], rx.at[me], at(z, ty, c_)
        )

    def merge1_start(k):
        merge1_copy(k, c).start()
        merge1_copy(k, 1 - c).start()

    loop(1, n, lambda k: merge1_start(n - k))
    merge1_copy(0, 1 - c).start()

    def gathered(k):
        for copy in hop1_copies(k) + hop2_copies(k):
            copy.wait_send()
        pass_on(k, 0).wait_send()
        pass_on(k, 1).wait_send()

    loop(1, n, gathered)
    loop(1, nx, lambda k: book_copy(k).wait_send())
    pass_on(0, 0).wait_send()
    pass_on(0, 1).wait_send()
    hand_cands.wait_send()

    def from1(k, c_):
        t = c_ * n + near(y, k, n)
        rcopy(tiles.at[t], got1.at[t], sx.at[t], rx.at[t], sibling).wait_recv()
        return got1[t]

    merged = lax.fori_loop(
        1, n,
        lambda k, acc: jnp.maximum(acc, jnp.maximum(from1(k, c), from1(k, 1 - c))),
        tiles[me],
    )
    merged = jnp.maximum(merged, from1(0, 1 - c))
    line[...] = merged

    def merge2_copy(k):
        tz = near(z, k, n)
        return rcopy(line.at[pl.ds(tz, 1)], got2.at[pl.ds(z, 1)], sy.at[k], ry.at[z], at(tz, y, c))

    loop(1, n, lambda k: merge2_copy(n - k).start())

    def merge1_sent(k):
        merge1_copy(k, c).wait_send()
        merge1_copy(k, 1 - c).wait_send()

    loop(1, n, merge1_sent)
    merge1_copy(0, 1 - c).wait_send()

    def from2(k, acc):
        tz = near(z, k, n)
        row = got2.at[pl.ds(tz, 1)]
        rcopy(row, row, sy.at[k], ry.at[tz], sibling).wait_recv()
        return jnp.maximum(acc, got2[pl.ds(tz, 1)])

    final = lax.fori_loop(1, n, from2, line[pl.ds(z, 1)])
    row_out[...] = final
    loop(1, n, lambda k: merge2_copy(k).wait_send())


def on_device(
    queries, candidates, codebook, bucket_weights, centroid_ids, residual_codes, passage_lengths, sizes
):
    n, nx = sizes
    query_len, width = queries.shape[2:]
    n_cand = candidates.shape[2]
    quarter = codebook.shape[0]
    n_pass, pass_len = centroid_ids.shape
    n_query = CORES * n * n
    tile_width = CORES * n * HALF
    vmem = pl.BlockSpec(memory_space=pltpu.VMEM)
    hbm = pl.BlockSpec(memory_space=pltpu.HBM)
    dma = pltpu.SemaphoreType.DMA
    f32, bf16, i32 = jnp.float32, jnp.bfloat16, jnp.int32
    row = pl.pallas_call(
        functools.partial(kernel, n, nx),
        out_shape=jax.ShapeDtypeStruct((1, 128), f32),
        in_specs=[hbm] * 7,
        out_specs=vmem,
        scratch_shapes=[
            pltpu.VMEM((query_len, width), bf16),
            pltpu.VMEM((1, n_cand), i32),
            pltpu.SMEM(bucket_weights.shape, f32),
            pltpu.SMEM(passage_lengths.shape, i32),
            pltpu.SMEM(centroid_ids.shape, i32),
            pltpu.VMEM((nx * quarter, width), bf16),
            pltpu.VMEM((nx * quarter, width), f32),
            pltpu.VMEM((2 * n_query, HALF, width), bf16),
            pltpu.VMEM(residual_codes.shape, i32),
            pltpu.VMEM(residual_codes.shape, f32),
            pltpu.VMEM((n_pass * pass_len, width), f32),
            pltpu.VMEM((n_pass * pass_len, width), bf16),
            pltpu.VMEM((2 * n, 8, tile_width), f32),
            pltpu.VMEM((n_pass, SLOTS * 2 * HALF), f32),
            pltpu.VMEM((1, 128), i32),
            pltpu.VMEM((n, 1, 128), i32),
            pltpu.VMEM((CORES * n, n, 128), i32),
            pltpu.VMEM((n_pass, n_query), f32),
            pltpu.VMEM((n_pass, 128), i32),
            pltpu.SMEM((n_pass, 128), i32),
            pltpu.VMEM((CORES * n, n, 128), f32),
            pltpu.VMEM((CORES * n, n, 128), f32),
            pltpu.VMEM((n, 128), f32),
            pltpu.VMEM((n, 128), f32),
            dma((9,)),
            dma((2, n)), dma((2, n)),
            dma((2, n)), dma((2, n)),
            dma((2, n)), dma((2, n)),
            dma((n,)), dma((n,)),
            dma((n,)), dma((n,)),
            dma((1,)), dma((1,)),
            dma((nx,)), dma((nx,)),
            dma((CORES * n,)), dma((CORES * n,)),
            dma((n,)), dma((n,)),
        ],
        compiler_params=pltpu.CompilerParams(
            collective_id=0, has_side_effects=True, vmem_limit_bytes=60 << 20
        ),
        cost_estimate=pl.CostEstimate(flops=4 << 30, bytes_accessed=2 << 20, transcendentals=0),
        name="late_interaction",
    )(
        queries.reshape(query_len, width), candidates.reshape(1, n_cand), bucket_weights,
        passage_lengths, centroid_ids, codebook, residual_codes,
    )
    row = row.reshape(1, 1, 128)
    return row[:, :, n_cand : n_cand + query_len], row[:, :, 0:n_cand]


def solution(mesh):
    from jax.sharding import PartitionSpec as P

    nx = mesh.shape["rep"]
    n = math.isqrt(mesh.shape["shard"] // CORES)
    in_specs = (
        P("rep", "shard", None, None),
        P("rep", "shard", None),
        P(("shard", "rep"), None),
        P(),
        P("shard", None),
        P("shard", None, None),
        P("shard"),
    )
    out_specs = (P("rep", "shard", None), P("rep", "shard", None))
    return jax.shard_map(
        functools.partial(on_device, sizes=(n, nx)),
        mesh=mesh, in_specs=in_specs, out_specs=out_specs, check_vma=False,
    )
```

```python
import functools
import math

import jax
import jax.numpy as jnp
from jax import lax
from jax.experimental import pallas as pl
from jax.experimental.pallas import tpu as pltpu

FAR_BELOW = -1e30
MESH = pl.DeviceIdType.MESH
CORES = 2
SLOTS = 8
HALF = 16
DIMS = (((1,), (1,)), ((), ()))


def kernel(
    n, nx, query_hbm, cand_hbm, weight_hbm, length_hbm, id_hbm, book_hbm, code_hbm,
    row_out,
    query_ref, cand_ref, weight_ref, length_ref, id_ref,
    book, book32, toks, codes, extra32, fetched, emb, best_acc, pair_best,
    cand_row, cand_line, cand_all, hits, slot_vec, slot_smem, tiles, got1, line, got2,
    local_sem, s1, r1, s2, r2, s3, r3, sc1, rc1, sc2, rc2, sc3, rc3, sb, rb, sx, rx, sy, ry,
):
    quarter = book_hbm.shape[0]
    n_pass, pass_len = id_ref.shape
    n_cand = cand_ref.shape[1]
    side = CORES * n
    n_blocks = n * side
    n_query = CORES * n * n
    width = side * HALF
    lane_half = n * HALF

    shard = lax.axis_index("shard")
    rep = lax.axis_index("rep")
    c = lax.rem(shard, CORES)
    y = lax.rem(shard // CORES, n)
    z = shard // (CORES * n)

    def at(z_, y_, c_):
        return {"shard": (z_ * n + y_) * CORES + c_, "rep": rep}

    def near(me, k, count):
        step = (k + 1) // 2
        return lax.rem(jnp.where(lax.rem(k, 2) == 1, me + step, me + count - step), count)

    def rcopy(src, dst, send, recv, dev):
        return pltpu.make_async_remote_copy(
            src_ref=src, dst_ref=dst, send_sem=send, recv_sem=recv,
            device_id=dev, device_id_type=MESH,
        )

    sibling = at(z, y, 1 - c)

    def loop(low, high, body):
        def step(k, carry):
            body(k)
            return carry
        lax.fori_loop(low, high, step, 0)

    def blocks_a(z_, c_):
        return toks.at[pl.ds((z_ * CORES + c_) * n, n)]

    def blocks_b(y_, c_):
        return toks.at[pl.ds(n_blocks + (y_ * CORES + c_) * n, n)]

    own_rows = pl.ds(pl.multiple_of(rep * quarter, quarter), quarter)
    load_book = pltpu.make_async_copy(book_hbm, book.at[own_rows], local_sem.at[0])
    load_codes = pltpu.make_async_copy(code_hbm, codes, local_sem.at[1])
    barrier = pltpu.get_barrier_semaphore()

    def greet(dev):
        pl.semaphore_signal(barrier, inc=1, device_id=dev, device_id_type=MESH)

    def greet_line(k):
        greet(at(z, near(y, k, n), c))
        greet(at(z, near(y, k, n), 1 - c))
        greet(at(near(z, k, n), y, c))

    loop(1, n, lambda k: greet_line(n - k))
    loop(1, nx, lambda k: greet({"shard": shard, "rep": near(rep, k, nx)}))
    greet(sibling)

    small = [
        pltpu.make_async_copy(source, target, local_sem.at[4 + i])
        for i, (source, target) in enumerate((
            (query_hbm, query_ref), (cand_hbm, cand_ref), (weight_hbm, weight_ref),
            (length_hbm, length_ref), (id_hbm, id_ref),
        ))
    ]
    for copy in small:
        copy.start()
    load_book.start()
    load_codes.start()
    for copy in small:
        copy.wait()
    toks[(z * CORES + c) * n + y] = query_ref[0:HALF]
    toks[n_blocks + (y * CORES + c) * n + z] = query_ref[HALF : 2 * HALF]
    cand_row[...] = jnp.full(cand_row.shape, -1, jnp.int32)
    cand_row[:, 0:n_cand] = cand_ref[...]
    cand_line[pl.ds(y, 1)] = cand_row[...].reshape(1, 1, 128)

    pl.semaphore_wait(barrier, 3 * (n - 1) + nx)

    def hop1_copies(k):
        ty, tz = near(y, k, n), near(z, k, n)
        block_a = toks.at[(z * CORES + c) * n + y]
        block_b = toks.at[n_blocks + (y * CORES + c) * n + z]
        return (
            rcopy(cand_line.at[y], cand_line.at[y], sc1.at[k], rc1.at[y], at(z, ty, c)),
            rcopy(block_a, block_a, s1.at[0, k], r1.at[0, y], at(z, ty, c)),
            rcopy(block_b, block_b, s1.at[1, k], r1.at[1, z], at(tz, y, c)),
        )

    def book_copy(k):
        return rcopy(
            book_hbm, book.at[own_rows], sb.at[k], rb.at[rep],
            {"shard": shard, "rep": near(rep, k, nx)},
        )

    def hop1_start(k):
        for copy in hop1_copies(k):
            copy.start()

    loop(1, n, lambda k: hop1_start(n - k))
    loop(1, nx, lambda k: book_copy(k).start())

    load_codes.wait()

    def residual(p):
        part = codes[p]
        value = jnp.zeros(part.shape, jnp.float32)
        for level in range(weight_ref.shape[0]):
            value = jnp.where(part == level, weight_ref[level], value)
        extra32[p] = value

    loop(0, n_pass, residual)

    def hop1_wait(k):
        ty, tz = near(y, k, n), near(z, k, n)
        block_a = toks.at[(z * CORES + c) * n + ty]
        block_b = toks.at[n_blocks + (y * CORES + c) * n + tz]
        rcopy(cand_line.at[ty], cand_line.at[ty], sc1.at[k], rc1.at[ty], sibling).wait_recv()
        rcopy(block_a, block_a, s1.at[0, k], r1.at[0, ty], sibling).wait_recv()
        rcopy(block_b, block_b, s1.at[1, k], r1.at[1, tz], sibling).wait_recv()

    loop(1, n, hop1_wait)

    def cand_slab(z_, c_):
        return cand_all.at[pl.ds(c_ * n, n), pl.ds(z_, 1)]

    def hop2_copies(k):
        ty, tz = near(y, k, n), near(z, k, n)
        return (
            rcopy(blocks_a(z, c), blocks_a(z, c), s2.at[0, k], r2.at[0, z], at(tz, y, c)),
            rcopy(blocks_b(y, c), blocks_b(y, c), s2.at[1, k], r2.at[1, y], at(z, ty, c)),
            rcopy(cand_line, cand_slab(z, c), sc2.at[k], rc2.at[z], at(tz, y, c)),
        )

    def hop2_start(k):
        for copy in hop2_copies(k):
            copy.start()

    loop(1, n, hop2_start)
    own_cands = pltpu.make_async_copy(cand_line, cand_slab(z, c), local_sem.at[2])
    own_cands.start()

    def pass_on(k, half):
        if half == 0:
            zk = near(z, k, n)
            return rcopy(blocks_a(zk, c), blocks_a(zk, c), s3.at[0, k], r3.at[0, zk], sibling)
        yk = near(y, k, n)
        return rcopy(blocks_b(yk, c), blocks_b(yk, c), s3.at[1, k], r3.at[1, yk], sibling)

    pass_on(0, 0).start()
    pass_on(0, 1).start()
    own_cands.wait()

    def span_of(r):
        return pl.ds(pl.multiple_of(r * quarter, quarter), quarter)

    def best_of(tile, r):
        token = toks[pl.ds(tile * side, side)].reshape(width, toks.shape[2])
        scored = lax.dot_general(book[span_of(r)], token, DIMS, preferred_element_type=jnp.float32)
        return jnp.max(scored.reshape(quarter // 8, 8, width), axis=0)

    def widen(r):
        book32[span_of(r)] = book[span_of(r)].astype(jnp.float32)

    def take_quarter(k):
        r = near(rep, k, nx)
        span = book.at[span_of(r)]
        rcopy(book_hbm, span, sb.at[k], rb.at[r], sibling).wait_recv()
        widen(r)

    def pair(k):
        zk, yk = near(z, k, n), near(y, k, n)
        other_a, other_b = blocks_a(zk, 1 - c), blocks_b(yk, 1 - c)
        rcopy(other_a, other_a, s3.at[0, k], r3.at[0, zk], sibling).wait_recv()
        rcopy(other_b, other_b, s3.at[1, k], r3.at[1, yk], sibling).wait_recv()
        for tile in (zk, n + yk):
            top = best_of(tile, rep)
            for j in range(1, nx - 1):
                top = jnp.maximum(top, best_of(tile, near(rep, j, nx)))
            best_acc[tile] = top

    def forward(k):
        zk, yk = near(z, k, n), near(y, k, n)
        rcopy(blocks_a(zk, c), blocks_a(zk, c), s2.at[0, k], r2.at[0, zk], sibling).wait_recv()
        pass_on(k, 0).start()
        rcopy(blocks_b(yk, c), blocks_b(yk, c), s2.at[1, k], r2.at[1, yk], sibling).wait_recv()
        pass_on(k, 1).start()

    load_book.wait()
    widen(rep)
    loop(1, nx - 1, take_quarter)
    pair(0)
    forward(1)

    if n > 2:
        forward(2)

    def arrive(k):
        forward(k)
        pair(k - 2)

    loop(3, n, arrive)

    def cands_wait(k):
        zk = near(z, k, n)
        rcopy(cand_line, cand_slab(zk, c), sc2.at[k], rc2.at[zk], sibling).wait_recv()

    loop(1, n, cands_wait)

    def cand_core(c_):
        return cand_all.at[pl.ds(c_ * n, n)]

    hand_cands = rcopy(cand_core(c), cand_core(c), sc3.at[0], rc3.at[0], sibling)
    hand_cands.start()
    loop(max(1, n - 2), n, pair)

    rcopy(cand_core(1 - c), cand_core(1 - c), sc3.at[0], rc3.at[0], sibling).wait_recv()
    cand_t = jnp.transpose(cand_all[...].reshape(n_query, 128))[0:n_cand]
    first_pass = shard * n_pass
    for p in range(n_pass):
        hits[p : p + 1, :] = jnp.max(
            jnp.where(cand_t == first_pass + p, 1.0, 0.0), axis=0, keepdims=True
        )
    hit = hits[...]
    before = (
        lax.broadcasted_iota(jnp.int32, (n_query, n_query), 0)
        < lax.broadcasted_iota(jnp.int32, (n_query, n_query), 1)
    ).astype(jnp.bfloat16)
    rank = jnp.dot(hit.astype(jnp.bfloat16), before, preferred_element_type=jnp.float32)
    rank = jnp.where(hit > 0.5, rank, -1.0)
    bits = n.bit_length() - 1
    q_index = lax.broadcasted_iota(jnp.int32, (n_pass, n_query), 1)
    q_z = q_index & (n - 1)
    q_y = (q_index >> bits) & (n - 1)
    q_c = q_index >> (2 * bits)
    at_a = ((q_z * CORES + q_c) * n + q_y).astype(jnp.float32)
    at_b = ((q_y * CORES + q_c) * n + q_z + n_blocks).astype(jnp.float32)
    lane = lax.broadcasted_iota(jnp.int32, (n_pass, 128), 1)
    slots = jnp.zeros((n_pass, 128), jnp.float32)
    for k in range(SLOTS):
        mine = rank == float(k)
        slots = jnp.where(
            lane == k, jnp.sum(jnp.where(mine, at_a, 0.0), axis=1, keepdims=True), slots
        )
        slots = jnp.where(
            lane == SLOTS + k, jnp.sum(jnp.where(mine, at_b, 0.0), axis=1, keepdims=True), slots
        )
    slot_vec[...] = slots.astype(jnp.int32)
    to_smem = pltpu.make_async_copy(slot_vec, slot_smem, local_sem.at[3])
    to_smem.start()

    take_quarter(nx - 1)

    def fetch(p):
        for u in range(pass_len):
            fetched[pl.ds(p * pass_len + u, 1)] = book32[pl.ds(id_ref[p, u], 1)]

    def decode(p):
        fetch(p)
        span = pl.ds(pl.multiple_of(p * pass_len, pass_len), pass_len)
        emb[span] = (fetched[span] + extra32[p]).astype(jnp.bfloat16)

    loop(0, n_pass, decode)

    last = near(rep, nx - 1, nx)
    for tile in range(2 * n):
        best_acc[tile] = jnp.maximum(best_acc[tile], best_of(tile, last))
    to_smem.wait()

    slot_iota = lax.broadcasted_iota(jnp.int32, (pass_len, SLOTS * 2 * HALF), 0)

    def score(i):
        for u in range(8):
            p = i * 8 + u
            parts = []
            for k in range(SLOTS):
                parts.append(toks[jnp.clip(slot_smem[p, k], 0, n_blocks - 1)])
                parts.append(
                    toks[jnp.clip(slot_smem[p, SLOTS + k], n_blocks, 2 * n_blocks - 1)]
                )
            picked = jnp.concatenate(parts, axis=0)
            span = pl.ds(pl.multiple_of(p * pass_len, pass_len), pass_len)
            similar = lax.dot_general(
                emb[span], picked, DIMS, preferred_element_type=jnp.float32
            )
            similar = jnp.where(slot_iota < length_ref[p], similar, FAR_BELOW)
            pair_best[pl.ds(p, 1)] = jnp.max(similar, axis=0, keepdims=True)

    loop(0, n_pass // 8, score)

    tok_of = lax.broadcasted_iota(jnp.int32, (SLOTS * 2 * HALF, 128), 0) >> 5
    col_of = lax.broadcasted_iota(jnp.int32, (SLOTS * 2 * HALF, 128), 1)
    ones = (tok_of == col_of).astype(jnp.float32)
    slot_score = jnp.dot(
        pair_best[...], ones, preferred_element_type=jnp.float32,
        precision=lax.Precision.HIGHEST,
    )
    table = jnp.zeros((n_pass, n_query), jnp.float32)
    for k in range(SLOTS):
        table = jnp.where(rank == float(k), slot_score[:, k : k + 1], table)
    chosen = jnp.full((n_cand, n_query), FAR_BELOW, jnp.float32)
    for p in range(n_pass):
        chosen = jnp.where(cand_t == first_pass + p, table[p : p + 1, :], chosen)
    chosen = jnp.transpose(
        jnp.concatenate([chosen, jnp.full((128 - n_cand, n_query), FAR_BELOW, jnp.float32)], axis=0)
    )

    best = jnp.max(best_acc[...], axis=1)
    row_of = lax.broadcasted_iota(jnp.int32, (n, 128), 0)
    lane_of = lax.broadcasted_iota(jnp.int32, (n, 128), 1)
    in_a = (lane_of >= n_cand) & (lane_of < n_cand + HALF)
    in_b = (lane_of >= n_cand + HALF) & (lane_of < n_cand + 2 * HALF)

    def fit(part):
        if lane_half == 128:
            return part
        return jnp.concatenate([part, jnp.full((n, 128 - lane_half), FAR_BELOW, jnp.float32)], axis=1)

    me = c * n + y

    def merge1_copy(k, c_):
        ty = near(y, k, n)
        return rcopy(
            tiles.at[c_ * n + ty], got1.at[me], sx.at[c_ * n + ty], rx.at[me], at(z, ty, c_)
        )

    for c_ in range(CORES):
        cols = slice(c_ * lane_half, (c_ + 1) * lane_half)
        best_a = fit(best[0:n, cols])
        best_b = fit(best[n : 2 * n, cols])
        for y_ in range(n):
            shift = (n_cand - y_ * HALF) % 128
            part_a = pltpu.roll(best_a, shift, 1) if shift else best_a
            part_b = jnp.where(
                (lane_of >> 4) == row_of, jnp.broadcast_to(best_b[y_ : y_ + 1], (n, 128)), FAR_BELOW
            )
            for step in (64, 32, 16):
                part_b = jnp.maximum(part_b, pltpu.roll(part_b, step, 1))
            t = c_ * n + y_
            tile = chosen[t * n : (t + 1) * n]
            tiles[t] = jnp.where(in_a, part_a, jnp.where(in_b, part_b, tile))
        loop(1, n, lambda k: merge1_copy(n - k, c_).start())
        pl.when(c != c_)(lambda: merge1_copy(0, c_).start())

    def gathered(k):
        for copy in hop1_copies(k) + hop2_copies(k):
            copy.wait_send()
        pass_on(k, 0).wait_send()
        pass_on(k, 1).wait_send()

    loop(1, n, gathered)
    loop(1, nx, lambda k: book_copy(k).wait_send())
    pass_on(0, 0).wait_send()
    pass_on(0, 1).wait_send()
    hand_cands.wait_send()

    def from1(k, c_):
        t = c_ * n + near(y, k, n)
        rcopy(tiles.at[t], got1.at[t], sx.at[t], rx.at[t], sibling).wait_recv()
        return got1[t]

    merged = lax.fori_loop(
        1, n,
        lambda k, acc: jnp.maximum(acc, jnp.maximum(from1(k, c), from1(k, 1 - c))),
        tiles[me],
    )
    merged = jnp.maximum(merged, from1(0, 1 - c))
    line[...] = merged

    def merge2_copy(k):
        tz = near(z, k, n)
        return rcopy(line.at[pl.ds(tz, 1)], got2.at[pl.ds(z, 1)], sy.at[k], ry.at[z], at(tz, y, c))

    loop(1, n, lambda k: merge2_copy(n - k).start())

    def merge1_sent(k):
        merge1_copy(k, c).wait_send()
        merge1_copy(k, 1 - c).wait_send()

    loop(1, n, merge1_sent)
    merge1_copy(0, 1 - c).wait_send()

    def from2(k, acc):
        tz = near(z, k, n)
        row = got2.at[pl.ds(tz, 1)]
        rcopy(row, row, sy.at[k], ry.at[tz], sibling).wait_recv()
        return jnp.maximum(acc, got2[pl.ds(tz, 1)])

    final = lax.fori_loop(1, n, from2, line[pl.ds(z, 1)])
    row_out[...] = final
    loop(1, n, lambda k: merge2_copy(k).wait_send())


def on_device(
    queries, candidates, codebook, bucket_weights, centroid_ids, residual_codes, passage_lengths, sizes
):
    n, nx = sizes
    query_len, width = queries.shape[2:]
    n_cand = candidates.shape[2]
    quarter = codebook.shape[0]
    n_pass, pass_len = centroid_ids.shape
    n_query = CORES * n * n
    tile_width = CORES * n * HALF
    vmem = pl.BlockSpec(memory_space=pltpu.VMEM)
    hbm = pl.BlockSpec(memory_space=pltpu.HBM)
    dma = pltpu.SemaphoreType.DMA
    f32, bf16, i32 = jnp.float32, jnp.bfloat16, jnp.int32
    row = pl.pallas_call(
        functools.partial(kernel, n, nx),
        out_shape=jax.ShapeDtypeStruct((1, 128), f32),
        in_specs=[hbm] * 7,
        out_specs=vmem,
        scratch_shapes=[
            pltpu.VMEM((query_len, width), bf16),
            pltpu.VMEM((1, n_cand), i32),
            pltpu.SMEM(bucket_weights.shape, f32),
            pltpu.SMEM(passage_lengths.shape, i32),
            pltpu.SMEM(centroid_ids.shape, i32),
            pltpu.VMEM((nx * quarter, width), bf16),
            pltpu.VMEM((nx * quarter, width), f32),
            pltpu.VMEM((2 * n_query, HALF, width), bf16),
            pltpu.VMEM(residual_codes.shape, i32),
            pltpu.VMEM(residual_codes.shape, f32),
            pltpu.VMEM((n_pass * pass_len, width), f32),
            pltpu.VMEM((n_pass * pass_len, width), bf16),
            pltpu.VMEM((2 * n, 8, tile_width), f32),
            pltpu.VMEM((n_pass, SLOTS * 2 * HALF), f32),
            pltpu.VMEM((1, 128), i32),
            pltpu.VMEM((n, 1, 128), i32),
            pltpu.VMEM((CORES * n, n, 128), i32),
            pltpu.VMEM((n_pass, n_query), f32),
            pltpu.VMEM((n_pass, 128), i32),
            pltpu.SMEM((n_pass, 128), i32),
            pltpu.VMEM((CORES * n, n, 128), f32),
            pltpu.VMEM((CORES * n, n, 128), f32),
            pltpu.VMEM((n, 128), f32),
            pltpu.VMEM((n, 128), f32),
            dma((9,)),
            dma((2, n)), dma((2, n)),
            dma((2, n)), dma((2, n)),
            dma((2, n)), dma((2, n)),
            dma((n,)), dma((n,)),
            dma((n,)), dma((n,)),
            dma((1,)), dma((1,)),
            dma((nx,)), dma((nx,)),
            dma((CORES * n,)), dma((CORES * n,)),
            dma((n,)), dma((n,)),
        ],
        compiler_params=pltpu.CompilerParams(
            collective_id=0, has_side_effects=True, vmem_limit_bytes=60 << 20
        ),
        cost_estimate=pl.CostEstimate(flops=4 << 30, bytes_accessed=2 << 20, transcendentals=0),
        name="late_interaction",
    )(
        queries.reshape(query_len, width), candidates.reshape(1, n_cand), bucket_weights,
        passage_lengths, centroid_ids, codebook, residual_codes,
    )
    row = row.reshape(1, 1, 128)
    return row[:, :, n_cand : n_cand + query_len], row[:, :, 0:n_cand]


def solution(mesh):
    from jax.sharding import PartitionSpec as P

    nx = mesh.shape["rep"]
    n = math.isqrt(mesh.shape["shard"] // CORES)
    in_specs = (
        P("rep", "shard", None, None),
        P("rep", "shard", None),
        P(("shard", "rep"), None),
        P(),
        P("shard", None),
        P("shard", None, None),
        P("shard"),
    )
    out_specs = (P("rep", "shard", None), P("rep", "shard", None))
    return jax.shard_map(
        functools.partial(on_device, sizes=(n, nx)),
        mesh=mesh, in_specs=in_specs, out_specs=out_specs, check_vma=False,
    )
```
